256 devices in a mesh: pipe: 4 (over x_hi, core), tensor: 16 (over x_lo, z), dp: 4 (over y).
Axes of the slice: x: 4 (x_hi: 2, x_lo: 2; x = x_hi * 2 + x_lo), y: 4, z: 8, core: 2. Of those that a mesh axis runs over, the one named last changes fastest.
Arguments:
- inputs: bfloat16 [2, 256, 4096], P(None, 'dp'), may hold values from -6 to 6
- layer_gain: float32 [4, 4096], P('pipe'), may hold values from 0.5 to 1.5
- up_weight: bfloat16 [4, 4096, 14336], P('pipe', 'dp', 'tensor'), may hold values from -0.09375 to 0.09375
- down_weight: bfloat16 [4, 14336, 4096], P('pipe', 'tensor', 'dp'), may hold values from -0.046875 to 0.046875
- final_gain: float32 [4096], replicated, may hold values from 0.5 to 1.5
- value_head: bfloat16 [4096], replicated, may hold values from -6 to 6
- q_head: bfloat16 [4096, 65536], P(None, ('pipe', 'tensor', 'dp')), may hold values from -620 to 620
- target_head: bfloat16 [4096, 65536], P(None, ('pipe', 'tensor', 'dp')), may hold values from -18 to 18
- actions: int32 [2, 256], replicated, may hold values from 0 to 65535
- rewards: int32 [2, 256], replicated, may hold values from -2 to 2
- done: int32 [2, 256], replicated, may hold values 0 or 1
- order: int32 [2], replicated, may hold values from 0 to 1, each once
Outputs:
- state_values: float32 [2, 256], replicated
- advantages: float32 [2, 256], replicated
- td_errors: float32 [2, 256], replicated
- value_loss: float32 [], replicated
- q_loss: float32 [], replicated
- lse_grad: bfloat16 [4096, 65536], P(None, ('pipe', 'tensor', 'dp'))
The draws below stay inside these ranges and needn't reach their ends.
Inputs may be any that keep to these rules, and one draw needn't show every extreme that they name: `order`: each micro-batch once.
All inputs are finite; a program needn't handle non-finite values.
Results may differ from the reference program's by a relative error of at most 0.04.
Values may be sent and summed in bfloat16 or wider, within the bound.
A program may use at most 128 MiB of HBM per device.

```python
import jax
import jax.numpy as jnp
from jax import lax

D = 4096
FF = 14336
VQ = 65536
MB = 2
TOK_MB = 64
TOKS = 256
N_PIPE = 4


def draw_q_head(key, part):
    first = jax.random.fold_in(jax.random.fold_in(key, 17), 0)
    return jnp.clip(jax.random.normal(first, (D, VQ), jnp.float32) * 3.0, -18.0, 18.0).astype(jnp.bfloat16)


def touch_ends(drawn, own_key, low, high):
    extent = drawn.shape
    spot = [jax.random.randint(jax.random.fold_in(own_key, axis), (), 0, extent[axis]) for axis in range(len(extent))]
    drawn = drawn.at[tuple(spot)].set(low)
    longest = extent.index(max(extent))
    spot[longest] = (spot[longest] + 1) % extent[longest]
    return drawn.at[tuple(spot)].set(high)


def level_of(rng, extent, shards, low, largest):
    def one(position, shards_of):
        draws = jax.random.uniform(jax.random.fold_in(jax.random.fold_in(rng, 6), position), (shards_of,), jnp.float32, low / len(shards), largest / len(shards))
        return jnp.repeat(jnp.exp(draws), extent[position] // shards_of).reshape((-1,) + (1,) * (len(extent) - position - 1))

    level = one(*shards[0])
    for cut in shards[1:]:
        level = level * one(*cut)
    return level


def normal_values(key, dims, scale, reach, cuts=(), dtype=jnp.bfloat16):
    values = scale * jax.random.normal(key, dims, jnp.float32)
    if cuts:
        values = values * level_of(key, dims, cuts, -0.22, 0.18)
    return jnp.clip(values, -reach, reach).astype(dtype)


def setup_inputs(seed: int = 0) -> dict:
    key_list = jax.random.split(jax.random.key(seed), 13)
    return {
        "inputs": normal_values(key_list[0], (MB, TOKS, D), 1.0, 6.0, ((1, 4),)),
        "layer_gain": jnp.clip(1.0 + 0.1 * jax.random.normal(key_list[1], (N_PIPE, D), jnp.float32), 0.5, 1.5),
        "up_weight": normal_values(key_list[2], (N_PIPE, D, FF), D ** -0.5, 0.09375, ((0, 4), (1, 4), (2, 16))),
        "down_weight": normal_values(key_list[3], (N_PIPE, FF, D), FF ** -0.5, 0.046875, ((0, 4), (1, 16), (2, 4))),
        "final_gain": jnp.clip(1.0 + 0.1 * jax.random.normal(key_list[4], (D,), jnp.float32), 0.5, 1.5),
        "value_head": normal_values(key_list[5], (D,), 1.0, 6.0),
        "q_head": draw_q_head(jax.random.fold_in(key_list[12], 71), 0),
        "target_head": normal_values(key_list[7], (D, VQ), 3.0, 18.0, ((1, 256),)),
        "actions": touch_ends(jax.random.randint(key_list[8], (MB, TOKS), 0, VQ), jax.random.fold_in(key_list[8], 1), 0, VQ - 1).astype(jnp.int32),
        "rewards": touch_ends(jax.random.randint(key_list[9], (MB, TOKS), -2, 3), jax.random.fold_in(key_list[9], 1), -2, 2).astype(jnp.int32),
        "done": touch_ends((jax.random.randint(key_list[10], (MB, TOKS), 0, 8) < 1).astype(jnp.int32), jax.random.fold_in(key_list[10], 1), 0, 1),
        "order": jax.random.permutation(key_list[11], MB).astype(jnp.int32),
    }


EPS = 1e-05
GAMMA = 0.99
TAU = 0.7
ALPHA = 0.5

def normed(values, gain):
    wide = values.astype(jnp.float32)
    factor = lax.rsqrt(lax.optimization_barrier(jnp.mean(wide * wide, axis=-1, keepdims=True)) + EPS)
    return wide * factor * gain.astype(jnp.float32)

def block(states, gain, w_up, w_down):
    normal = normed(states, gain).astype(jnp.bfloat16)
    upper = jnp.dot(normal, w_up, preferred_element_type=jnp.float32)
    hidden = jax.nn.silu(upper).astype(jnp.bfloat16)
    return (states.astype(jnp.float32) + jnp.dot(hidden, w_down, preferred_element_type=jnp.float32)).astype(jnp.bfloat16)

def reference(inputs, layer_gain, up_weight, down_weight, final_gain, value_head, q_head, target_head, actions, rewards, done, order):
    chosen = jnp.take(inputs, order, axis=0)
    states = chosen.reshape(MB * TOKS, D)
    for section in range(N_PIPE):
        states = block(states, layer_gain[section], up_weight[section], down_weight[section])
    final = normed(states, final_gain).astype(jnp.bfloat16)
    action = jnp.take(actions, order, axis=0).reshape(-1).astype(jnp.int32)
    reward = jnp.take(rewards, order, axis=0).reshape(-1).astype(jnp.float32)
    finished = jnp.take(done, order, axis=0).reshape(-1).astype(jnp.float32)
    factor = D ** (-0.5)
    values = jnp.dot(final, value_head, preferred_element_type=jnp.float32) * factor
    logits = jnp.dot(final, q_head, preferred_element_type=jnp.float32) * factor
    top = lax.optimization_barrier(jnp.max(logits, axis=-1))
    total = lax.optimization_barrier(jnp.sum(jnp.exp(logits - top[:, None]), axis=-1))
    lse = top + jnp.log(total)
    column = lax.broadcasted_iota(jnp.int32, (1, VQ), 1)
    onehot = (action[:, None] == column).astype(jnp.float32)
    taken = lax.optimization_barrier(jnp.sum(logits * onehot, axis=-1))
    target_cols = jnp.take(target_head, action, axis=1)
    target_taken = lax.optimization_barrier(jnp.sum(final.astype(jnp.float32) * target_cols.T.astype(jnp.float32), axis=-1)) * factor
    windows = values.reshape(-1, TOK_MB)
    following = jnp.concatenate([windows[:, 1:], jnp.zeros((windows.shape[0], 1), jnp.float32)], axis=1).reshape(-1)
    bootstrap = 0.5 * reward + GAMMA * (1.0 - finished) * following
    td_value = taken - bootstrap
    advantage = target_taken - values
    weight = jnp.where(advantage < 0, 1.0 - TAU, TAU)
    value_loss = jnp.mean(weight * advantage * advantage)
    q_loss = jnp.mean(td_value * td_value + ALPHA * (lse - taken))
    probs = jnp.exp(logits - lse[:, None]).astype(jnp.bfloat16)
    scale = VQ * factor / (MB * TOKS)
    summed = lax.dot_general(final, probs, (((0,), (0,)), ((), ())), preferred_element_type=jnp.float32)
    lse_grad = (summed * scale).astype(jnp.bfloat16)
    shape = (MB, TOKS)
    return (values.reshape(shape), advantage.reshape(shape), td_value.reshape(shape), value_loss, q_loss, lse_grad)
```

```python
import jax
import jax.numpy as jnp
from jax import lax
from jax.experimental import pallas as pl
from jax.experimental.pallas import tpu as pltpu
from jax.sharding import PartitionSpec as P

VQ = 65536
EPS = 1e-05
GAMMA = 0.99
TAU = 0.7
ALPHA = 0.5

MB = 2
WIN = 64
ROWS = 256
D = 4096
DC = 1024
FT = 896
UW = 1024
NP, NT, ND, NZ = 4, 16, 4, 8
SUB = 16
HALF = 128
CH = 256
BF, F32 = jnp.bfloat16, jnp.float32
MESH = pl.DeviceIdType.MESH


def remote(src, dst, send, recv, dev):
    return pltpu.make_async_remote_copy(
        src_ref=src, dst_ref=dst, send_sem=send, recv_sem=recv, device_id=dev, device_id_type=MESH
    )


def loop(low, high, body):
    def step(i, carry):
        body(i)
        return carry

    lax.fori_loop(low, high, step, 0)


def trunk(
    order, acts, lgain, fgain, vhead, x_any, up_any, dn_any, q_any, tg_any,
    g_out, lt_out, st_out,
    xin, xs, sbuf, upw, dnw, qv, tv, usend, urecv, hbuf, dsend, drecv, osend, gbuf, gg,
    acc, acct, vacc, ssq, own, l1, own2, l2,
    lsem, isnd, ircv, usnd, urcv, hsnd, hrcv, dsnd, drcv, ssnd, srcv,
    zsnd, zrcv, fxsnd, fxrcv, fysnd, fyrcv, fcsnd, fcrcv, l1snd, l1rcv, l2snd, l2rcv,
):
    p, t, d = lax.axis_index("pipe"), lax.axis_index("tensor"), lax.axis_index("dp")
    xl, z = t // NZ, t % NZ

    def seg(i, n):
        return pl.ds(pl.multiple_of(i * n, n), n)

    loads = [
        pltpu.make_async_copy(up_any.at[0], upw, lsem.at[0]),
        pltpu.make_async_copy(dn_any.at[0], dnw, lsem.at[1]),
        pltpu.make_async_copy(q_any, qv, lsem.at[2]),
        pltpu.make_async_copy(tg_any, tv, lsem.at[3]),
    ]
    load_x = pltpu.make_async_copy(x_any, xin, lsem.at[4])

    def c_in(m, k):
        dd = (d + k) % ND
        return remote(
            xs.at[m, :, seg(dd, DC)], sbuf.at[m, seg(d, WIN), :], isnd.at[m, k], ircv.at[m, d], (p, t, dd)
        )

    def w_in(m, k):
        s = (d + k) % ND
        remote(xs.at[m, :, seg(s, DC)], sbuf.at[m, seg(s, WIN), :], isnd.at[m, k], ircv.at[m, s], (p, t, s)).wait_recv()

    def c_up(m, k):
        dd = (d + k) % ND
        return remote(usend.at[m, seg(dd, WIN), :], urecv.at[m, d], usnd.at[m, k], urcv.at[m, d], (p, t, dd))

    def w_up(m, k):
        s = (d + k) % ND
        remote(usend.at[m, seg(s, WIN), :], urecv.at[m, s], usnd.at[m, k], urcv.at[m, s], (p, t, s)).wait_recv()

    def c_hid(m, k):
        dd = (d + k) % ND
        part = hbuf.at[m, seg(d, WIN), :]
        return remote(part, part, hsnd.at[m, k], hrcv.at[m, d], (p, t, dd))

    def w_hid(m, k):
        s = (d + k) % ND
        part = hbuf.at[m, seg(s, WIN), :]
        remote(part, part, hsnd.at[m, k], hrcv.at[m, s], (p, t, s)).wait_recv()

    def c_down(m, k):
        tt = (t + k) % NT
        return remote(dsend.at[m, seg(tt, SUB), :], drecv.at[m, t], dsnd.at[m, k], drcv.at[m, t], (p, tt, d))

    def w_down(m, k):
        s = (t + k) % NT
        remote(dsend.at[m, seg(s, SUB), :], drecv.at[m, s], dsnd.at[m, k], drcv.at[m, s], (p, s, d)).wait_recv()

    def c_state(m, k):
        tt = (t + k) % NT
        return remote(
            osend.at[m], sbuf.at[m, seg(t, SUB), :], ssnd.at[m, k], srcv.at[m, t], (lax.rem(p + 1, NP), tt, d)
        )

    def w_state(m, k):
        s = (t + k) % NT
        remote(
            osend.at[m], sbuf.at[m, seg(s, SUB), :], ssnd.at[m, k], srcv.at[m, s], (lax.rem(p + 3, NP), s, d)
        ).wait_recv()

    def piece(m, tt):
        return gbuf.at[seg(m * NT + tt, SUB), seg(d, DC)]

    def c_z(m, k):
        tt = xl * NZ + (z + k) % NZ
        return remote(piece(m, t), piece(m, t), zsnd.at[m, k], zrcv.at[m, z], (p, tt, d))

    def w_z(m, k):
        zz = (z + k) % NZ
        tt = xl * NZ + zz
        remote(piece(m, tt), piece(m, tt), zsnd.at[m, k], zrcv.at[m, zz], (p, tt, d)).wait_recv()

    def block(m, b, dd):
        return gbuf.at[seg(m * 2 + b, HALF), seg(dd, DC)]

    def c_x(m, i):
        part = block(m, xl, d)
        across = (1 - xl) * NZ + z
        dev = ((3, across, d), (1, t, d), (1, across, d))[i]
        return remote(part, part, fxsnd.at[m, i], fxrcv.at[m, xl], dev)

    def w_x(m, b):
        part = block(m, b, d)
        remote(part, part, fxsnd.at[m, 0], fxrcv.at[m, b], (p, (1 - xl) * NZ + z, d)).wait_recv()

    def c_y(m, b, k):
        dd = (d + k) % ND
        part = block(m, b, d)
        return remote(part, part, fysnd.at[m, b, k], fyrcv.at[m, b, d], (p, t, dd))

    def w_y(m, b, k):
        s = (d + k) % ND
        part = block(m, b, s)
        remote(part, part, fysnd.at[m, b, k], fyrcv.at[m, b, s], (p, t, s)).wait_recv()

    def other_core():
        return (p + 1 - 2 * lax.rem(p, 2), t, d)

    def c_core(m, b, k):
        dd = (d + k) % ND
        part = block(m, b, dd)
        return remote(part, part, fcsnd.at[m, b, k], fcrcv.at[m, b, dd], other_core())

    def w_core(m, b, k):
        c_core(m, b, k).wait_recv()

    def c_one(k):
        tt = (t + k) % NT
        return remote(own, l1.at[t], l1snd.at[k], l1rcv.at[t], (p, tt, d))

    def w_one(k):
        s = (t + k) % NT
        remote(own, l1.at[s], l1snd.at[k], l1rcv.at[s], (p, s, d)).wait_recv()

    def c_two(k):
        mine = p * ND + d
        o = (mine + k) % (NP * ND)
        return remote(own2, l2.at[mine], l2snd.at[k], l2rcv.at[mine], (o // ND, t, o % ND))

    def w_two(k):
        s = (p * ND + d + k) % (NP * ND)
        remote(own2, l2.at[s], l2snd.at[k], l2rcv.at[s], (s // ND, t, s % ND)).wait_recv()

    first, last, carrier = p == 0, p == NP - 1, lax.rem(p, 2) == 1

    @pl.when(first)
    def _():
        load_x.start()

    for one in loads:
        one.start()

    @pl.when(first)
    def _():
        load_x.wait()

        def enter(m):
            xs[m] = xin[order[m]]
            loop(1, ND, lambda k: c_in(m, k).start())
            sbuf[m, seg(d, WIN), :] = xs[m, :, seg(d, DC)]

        loop(0, MB, enter)

    loads[0].wait()

    def up(m):
        @pl.when(first)
        def _():
            loop(1, ND, lambda k: w_in(m, k))

        @pl.when(p > 0)
        def _():
            loop(0, NT, lambda k: w_state(m, k))

        wide = sbuf[m].astype(F32)
        square = jnp.sum(wide * wide, axis=-1, keepdims=True)
        scaled = (wide * lgain[0:1, seg(d, DC)]).astype(BF)
        usend[m, :, :FT] = jnp.dot(scaled, upw[...], preferred_element_type=F32).astype(BF)
        high = square.astype(BF).astype(F32)
        lane = lax.broadcasted_iota(jnp.int32, (ROWS, UW - FT), 1)
        usend[m, :, FT:] = jnp.where(lane < (UW - FT) // 2, high, square - high).astype(BF)
        loop(1, ND, lambda k: c_up(m, k).start())

    loop(0, MB, up)

    def hidden(m):
        total = usend[m, seg(d, WIN), :].astype(F32)
        for k in range(1, ND):
            w_up(m, k)
            total = total + urecv[m, (d + k) % ND].astype(F32)
        square = total[:, FT : FT + 1] + total[:, (FT + UW) // 2 : (FT + UW) // 2 + 1]
        upper = total[:, :FT] * lax.rsqrt(square / D + EPS)
        hbuf[m, seg(d, WIN), :] = (upper / (1.0 + jnp.exp(-upper))).astype(BF)
        loop(1, ND, lambda k: c_hid(m, k).start())

    loop(0, MB, hidden)
    loads[1].wait()

    def down(m):
        loop(1, ND, lambda k: w_hid(m, k))
        dsend[m] = jnp.dot(hbuf[m], dnw[...], preferred_element_type=F32).astype(BF)
        loop(1, NT, lambda k: c_down(m, k).start())

    loop(0, MB, down)

    def reduce(m):
        def add(k, total):
            w_down(m, k)
            return total + drecv[m, (t + k) % NT].astype(F32)

        total = lax.fori_loop(1, NT, add, dsend[m, seg(t, SUB), :].astype(F32))
        osend[m] = (sbuf[m, seg(t, SUB), :].astype(F32) + total).astype(BF)

        @pl.when(p < NP - 1)
        def _():
            loop(0, NT, lambda k: c_state(m, k).start())

        @pl.when(last)
        def _():
            gbuf[seg(m * NT + t, SUB), seg(d, DC)] = osend[m]
            loop(1, NZ, lambda k: c_z(m, k).start())
            loop(1, NZ, lambda k: w_z(m, k))
            for i in range(3):
                c_x(m, i).start()
            loop(1, ND, lambda k: c_y(m, xl, k).start())
            c_core(m, xl, 0).start()

    loop(0, MB, reduce)

    @pl.when(carrier)
    def _():
        def across(m):
            def pass_on(b):
                @pl.when(jnp.logical_or(p == 1, b != xl))
                def _():
                    w_x(m, b)
                    loop(1, ND, lambda k: c_y(m, b, k).start())
                    c_core(m, b, 0).start()

            loop(0, 2, pass_on)

            def hand_over(b):
                def one(k):
                    w_y(m, b, k)
                    c_core(m, b, k).start()

                loop(1, ND, one)

            loop(0, 2, hand_over)

        loop(0, MB, across)

    loads[2].wait()
    loads[3].wait()
    offset = ((p * NT + t) * ND + d) * CH
    ids = offset + lax.broadcasted_iota(jnp.int32, (CH, ROWS), 0)
    wide_head = jnp.broadcast_to(vhead[...].astype(F32), (16, D)).astype(BF)
    vacc_head = wide_head

    def head(m):
        @pl.when(jnp.logical_not(carrier))
        def _():
            loop(0, 2, lambda b: loop(0, ND, lambda k: w_core(m, b, k)))

        for c in range(ND):
            wide = gbuf[seg(m, ROWS), c * DC : (c + 1) * DC].astype(F32)
            square = jnp.sum(wide * wide, axis=-1, keepdims=True)
            scaled = (wide * fgain[0:1, c * DC : (c + 1) * DC]).astype(BF)
            gg[seg(m, ROWS), c * DC : (c + 1) * DC] = scaled
            part = jnp.dot(scaled, qv[c * DC : (c + 1) * DC, :], preferred_element_type=F32)
            tpart = jnp.dot(scaled, tv[c * DC : (c + 1) * DC, :], preferred_element_type=F32)
            vpart = lax.dot_general(
                vacc_head[:, c * DC : (c + 1) * DC], scaled, (((1,), (1,)), ((), ())), preferred_element_type=F32
            )
            if c == 0:
                acc[...], acct[...], vacc[...], ssq[...] = part, tpart, vpart, jnp.broadcast_to(square, (ROWS, 128))
            else:
                acc[...] += part
                acct[...] += tpart
                vacc[...] += vpart
                ssq[...] += square
        write = pltpu.make_async_copy(gg.at[seg(m, ROWS), :], g_out.at[seg(m, ROWS), :], lsem.at[5 + m])
        write.start()
        factor = lax.rsqrt(ssq[...].T[0:1, :] / D + EPS)
        small = factor * D**-0.5
        logits = acc[...].T * small
        target = acct[...].T * small
        at = order[m]
        action = acts[0:1, :] + (acts[1:2, :] - acts[0:1, :]) * at
        hit = ids == action
        top = jnp.max(logits, axis=0, keepdims=True)
        cols = seg(m, ROWS)
        lt_out[:, cols] = logits
        own[0:1, cols] = top
        own[1:2, cols] = jnp.sum(jnp.exp(logits - top), axis=0, keepdims=True)
        own[2:3, cols] = jnp.sum(jnp.where(hit, logits, 0.0), axis=0, keepdims=True)
        own[3:4, cols] = jnp.sum(jnp.where(hit, target, 0.0), axis=0, keepdims=True)
        own[4:8, cols] = jnp.zeros((4, ROWS), F32)
        st_out[3:4, cols] = vacc[0:1, :] * small
        st_out[4:5, cols] = factor

    loop(0, MB, head)

    def combined(parts):
        top = jnp.max(parts[:, 0, :], axis=0, keepdims=True)
        total = jnp.sum(parts[:, 1, :] * jnp.exp(parts[:, 0, :] - top), axis=0, keepdims=True)
        taken = jnp.sum(parts[:, 2, :], axis=0, keepdims=True)
        target = jnp.sum(parts[:, 3, :], axis=0, keepdims=True)
        return top, total, taken, target

    loop(1, NT, lambda k: c_one(k).start())
    l1[t] = own[...]
    loop(1, NT, w_one)
    top, total, taken, target = combined(l1[...])
    own2[0:1, :] = top
    own2[1:2, :] = total
    own2[2:3, :] = taken
    own2[3:4, :] = target
    own2[4:8, :] = jnp.zeros((4, MB * ROWS), F32)
    loop(1, NP * ND, lambda k: c_two(k).start())
    l2[p * ND + d] = own2[...]
    loop(1, NP * ND, w_two)
    top, total, taken, target = combined(l2[...])
    st_out[0:1, :] = top + jnp.log(total)
    st_out[1:2, :] = taken
    st_out[2:3, :] = target
    st_out[5:8, :] = jnp.zeros((3, MB * ROWS), F32)

    def sent(m):
        @pl.when(first)
        def _():
            loop(1, ND, lambda k: c_in(m, k).wait_send())

        loop(1, ND, lambda k: c_up(m, k).wait_send())
        loop(1, ND, lambda k: c_hid(m, k).wait_send())
        loop(1, NT, lambda k: c_down(m, k).wait_send())

        @pl.when(p < NP - 1)
        def _():
            loop(0, NT, lambda k: c_state(m, k).wait_send())

        @pl.when(last)
        def _():
            loop(1, NZ, lambda k: c_z(m, k).wait_send())
            for i in range(3):
                c_x(m, i).wait_send()

        @pl.when(carrier)
        def _():
            def of_block(b):
                loop(1, ND, lambda k: c_y(m, b, k).wait_send())
                loop(0, ND, lambda k: c_core(m, b, k).wait_send())

            loop(0, 2, of_block)

        pltpu.make_async_copy(gg.at[seg(m, ROWS), :], g_out.at[seg(m, ROWS), :], lsem.at[5 + m]).wait()

    loop(0, MB, sent)
    loop(1, NT, lambda k: c_one(k).wait_send())
    loop(1, NP * ND, lambda k: c_two(k).wait_send())


def run_trunk(order, acts, lgain, fgain, vhead, x, up, dn, q, tg):
    vm, anyw = pl.BlockSpec(memory_space=pltpu.VMEM), pl.BlockSpec(memory_space=pl.ANY)
    sm = pl.BlockSpec(memory_space=pltpu.SMEM)
    dma = pltpu.SemaphoreType.DMA
    rows = MB * ROWS
    return pl.pallas_call(
        trunk,
        name="trunk",
        out_shape=(
            jax.ShapeDtypeStruct((rows, D), BF),
            jax.ShapeDtypeStruct((CH, rows), F32),
            jax.ShapeDtypeStruct((8, rows), F32),
        ),
        in_specs=[sm, vm, vm, vm, vm] + [anyw] * 5,
        out_specs=(anyw, vm, vm),
        scratch_shapes=[
            pltpu.VMEM((MB, WIN, D), BF),
            pltpu.VMEM((MB, WIN, D), BF),
            pltpu.VMEM((MB, ROWS, DC), BF),
            pltpu.VMEM((DC, FT), BF),
            pltpu.VMEM((FT, DC), BF),
            pltpu.VMEM((D, CH), BF),
            pltpu.VMEM((D, CH), BF),
            pltpu.VMEM((MB, ROWS, UW), BF),
            pltpu.VMEM((MB, ND, WIN, UW), BF),
            pltpu.VMEM((MB, ROWS, FT), BF),
            pltpu.VMEM((MB, ROWS, DC), BF),
            pltpu.VMEM((MB, NT, SUB, DC), BF),
            pltpu.VMEM((MB, SUB, DC), BF),
            pltpu.VMEM((rows, D), BF),
            pltpu.VMEM((rows, D), BF),
            pltpu.VMEM((ROWS, CH), F32),
            pltpu.VMEM((ROWS, CH), F32),
            pltpu.VMEM((16, ROWS), F32),
            pltpu.VMEM((ROWS, 128), F32),
            pltpu.VMEM((8, rows), F32),
            pltpu.VMEM((NT, 8, rows), F32),
            pltpu.VMEM((8, rows), F32),
            pltpu.VMEM((NP * ND, 8, rows), F32),
            dma((8,)),
            dma((MB, ND)), dma((MB, ND)),
            dma((MB, ND)), dma((MB, ND)),
            dma((MB, ND)), dma((MB, ND)),
            dma((MB, NT)), dma((MB, NT)),
            dma((MB, NT)), dma((MB, NT)),
            dma((MB, NZ)), dma((MB, NZ)),
            dma((MB, 4)), dma((MB, 2)),
            dma((MB, 2, ND)), dma((MB, 2, ND)),
            dma((MB, 2, ND)), dma((MB, 2, ND)),
            dma((NT,)), dma((NT,)),
            dma((NP * ND,)), dma((NP * ND,)),
        ],
        compiler_params=pltpu.CompilerParams(has_side_effects=True, vmem_limit_bytes=48 * 2**20),
    )(order, acts, lgain, fgain, vhead, x, up, dn, q, tg)


FB = 512


def finish(order, rewards, done, g, lt, st, val, adv, td, vloss, qloss, grad, probs):
    @pl.when(pl.program_id(0) == 0)
    def _():
        lse, taken, target, raw, factor = (st[i : i + 1, :] for i in range(5))
        probs[...] = (jnp.exp(lt[...] - lse) * factor).T.astype(BF)
        rows = MB * ROWS

        def chosen(ref):
            a, b = ref[0:1, :], ref[1:2, :]
            return jnp.concatenate([a + (b - a) * order[m] for m in range(MB)], axis=1).astype(F32)

        reward, finished = chosen(rewards), chosen(done)
        lane = lax.broadcasted_iota(jnp.int32, (1, rows), 1)
        following = jnp.where(lane % WIN == WIN - 1, 0.0, pltpu.roll(raw, rows - 1, 1))
        error = taken - (0.5 * reward + GAMMA * (1.0 - finished) * following)
        gain = target - raw
        weight = jnp.where(gain < 0, 1.0 - TAU, TAU)
        for m in range(MB):
            cols = slice(m * ROWS, (m + 1) * ROWS)
            val[m : m + 1, :] = raw[:, cols]
            adv[m : m + 1, :] = gain[:, cols]
            td[m : m + 1, :] = error[:, cols]
        vloss[...] = jnp.sum(weight * gain * gain, axis=1, keepdims=True) / rows
        qloss[...] = jnp.sum(error * error + ALPHA * (lse - taken), axis=1, keepdims=True) / rows

    product = lax.dot_general(g[...], probs[...], (((0,), (0,)), ((), ())), preferred_element_type=F32)
    grad[...] = (product * (VQ * D**-0.5 / (MB * ROWS))).astype(BF)


def run_finish(order, rewards, done, g, lt, st):
    rows = MB * ROWS

    def whole(*shape):
        return pl.BlockSpec(shape, lambda i: (0,) * len(shape))

    small = jax.ShapeDtypeStruct((MB, ROWS), F32)
    one = jax.ShapeDtypeStruct((1, 1), F32)
    return pl.pallas_call(
        finish,
        name="finish",
        grid=(D // FB,),
        out_shape=(small, small, small, one, one, jax.ShapeDtypeStruct((D, CH), BF)),
        in_specs=[
            pl.BlockSpec(memory_space=pltpu.SMEM),
            whole(MB, ROWS),
            whole(MB, ROWS),
            pl.BlockSpec((rows, FB), lambda i: (0, i)),
            whole(CH, rows),
            whole(8, rows),
        ],
        out_specs=(
            whole(MB, ROWS),
            whole(MB, ROWS),
            whole(MB, ROWS),
            whole(1, 1),
            whole(1, 1),
            pl.BlockSpec((FB, CH), lambda i: (i, 0)),
        ),
        scratch_shapes=[pltpu.VMEM((rows, CH), BF)],
        compiler_params=pltpu.CompilerParams(vmem_limit_bytes=32 * 2**20),
    )(order, rewards, done, g, lt, st)


def local(
    inputs, layer_gain, up_weight, down_weight, final_gain, value_head,
    q_head, target_head, actions, rewards, done, order,
):
    g, lt, st = run_trunk(
        order, actions, layer_gain, final_gain.reshape(1, D), value_head.reshape(1, D),
        inputs, up_weight, down_weight, q_head, target_head,
    )
    val, adv, td, vloss, qloss, grad = run_finish(order, rewards, done, g, lt, st)
    return val, adv, td, vloss.reshape(()), qloss.reshape(()), grad


def solution(mesh):
    in_specs = (
        P(None, "dp", None),
        P("pipe", None),
        P("pipe", "dp", "tensor"),
        P("pipe", "tensor", "dp"),
        P(),
        P(),
        P(None, ("pipe", "tensor", "dp")),
        P(None, ("pipe", "tensor", "dp")),
        P(),
        P(),
        P(),
        P(),
    )
    out_specs = (P(), P(), P(), P(), P(), P(None, ("pipe", "tensor", "dp")))
    return jax.shard_map(local, mesh=mesh, in_specs=in_specs, out_specs=out_specs, check_vma=False)
```

```python
import jax
import jax.numpy as jnp
from jax import lax
from jax.experimental import pallas as pl
from jax.experimental.pallas import tpu as pltpu
from jax.sharding import PartitionSpec as P

VQ = 65536
EPS = 1e-05
GAMMA = 0.99
TAU = 0.7
ALPHA = 0.5

MB = 2
MROWS = 256
WIN = 64
NC, ROWS = 4, 128
D = 4096
DC = 1024
FT = 896
UW = 1024
NP, NT, ND, NZ = 4, 16, 4, 8
SPLIT = 32
SUB, XC = 16, 512
VMEM = 63 * 2**20
CH = 256
BF, F32 = jnp.bfloat16, jnp.float32
MESH = pl.DeviceIdType.MESH


def remote(src, dst, send, recv, dev):
    return pltpu.make_async_remote_copy(
        src_ref=src, dst_ref=dst, send_sem=send, recv_sem=recv, device_id=dev, device_id_type=MESH
    )


def loop(low, high, body):
    def step(i, carry):
        body(i)
        return carry

    lax.fori_loop(low, high, step, 0)


def trunk(
    order_any, acts_any, lgain_any, fgain_any, vhead_any, x_any, up_any, dn_any, q_any, tg_any,
    g_out, lt_out, st_out,
    order, acts, lgain, fgain, vhead, xin, xs, sbuf, upw, dnw, qv, tv, usend, urecv, hbuf, dsend, drecv, osend,
    gbuf, gg, acc, acct, vacc, ssq, own, l1, own2, l2,
    lsem, gsem, isnd, ircv, usnd, urcv, hsnd, hrcv, dsnd, drcv, ssnd, srcv,
    f1snd, f1rcv, f2snd, f2rcv, fxsnd, fxrcv, fcsnd, fcrcv, l1snd, l1rcv, l2snd, l2rcv,
):
    p, t, d = lax.axis_index("pipe"), lax.axis_index("tensor"), lax.axis_index("dp")
    xl, z = t // NZ, t % NZ

    def seg(i, n):
        return pl.ds(pl.multiple_of(i * n, n), n)

    loads = [
        pltpu.make_async_copy(up_any.at[0], upw, lsem.at[0]),
        pltpu.make_async_copy(dn_any.at[0], dnw, lsem.at[1]),
        pltpu.make_async_copy(q_any, qv, lsem.at[2]),
        pltpu.make_async_copy(tg_any, tv, lsem.at[3]),
        pltpu.make_async_copy(fgain_any, fgain, lsem.at[4]),
        pltpu.make_async_copy(vhead_any, vhead, lsem.at[5]),
        pltpu.make_async_copy(acts_any, acts, lsem.at[6]),
    ]
    load_x = pltpu.make_async_copy(x_any, xin, lsem.at[7])
    load_order = pltpu.make_async_copy(order_any, order, lsem.at[8])
    load_gain = pltpu.make_async_copy(lgain_any, lgain, lsem.at[9])


    def entry(m, s):
        return sbuf.at[2 * m + s // 2, seg(s % 2, WIN), :]

    def c_in(m, k):
        dd = (d + k) % ND
        return remote(xs.at[m, :, seg(dd, DC)], entry(m, d), isnd.at[m, k], ircv.at[m, d], (p, t, dd))

    def w_in(m, s):
        remote(xs.at[m, :, seg(s, DC)], entry(m, s), isnd.at[m, 0], ircv.at[m, s], (p, t, s)).wait_recv()

    def c_up(c, k):
        dd = (d + k) % ND
        return remote(usend.at[c, seg(dd, SPLIT), :], urecv.at[c, d], usnd.at[c, k], urcv.at[c, d], (p, t, dd))

    def w_up(c, k):
        s = (d + k) % ND
        remote(usend.at[c, seg(s, SPLIT), :], urecv.at[c, s], usnd.at[c, k], urcv.at[c, s], (p, t, s)).wait_recv()

    def c_hid(c, k):
        dd = (d + k) % ND
        part = hbuf.at[c, seg(d, SPLIT), :]
        return remote(part, part, hsnd.at[c, k], hrcv.at[c, d], (p, t, dd))

    def w_hid(c, k):
        s = (d + k) % ND
        part = hbuf.at[c, seg(s, SPLIT), :]
        remote(part, part, hsnd.at[c, k], hrcv.at[c, s], (p, t, s)).wait_recv()

    def tile(ref, c, tt):
        return ref.at[c, seg(tt % NZ, SUB), seg(tt // NZ, XC)]

    def c_down(c, k):
        tt = (t + k) % NT
        return remote(tile(dsend, c, tt), drecv.at[c, t], dsnd.at[c, k], drcv.at[c, t], (p, tt, d))

    def w_down(c, k):
        s = (t + k) % NT
        remote(tile(dsend, c, s), drecv.at[c, s], dsnd.at[c, k], drcv.at[c, s], (p, s, d)).wait_recv()

    def c_state(c, k):
        tt = (t + k) % NT
        return remote(
            osend.at[c], tile(sbuf, c, t), ssnd.at[c, k], srcv.at[c, t], (lax.rem(p + 1, NP), tt, d)
        )

    def w_state(c, k):
        s = (t + k) % NT
        remote(
            osend.at[c], tile(sbuf, c, s), ssnd.at[c, k], srcv.at[c, s], (lax.rem(p + 3, NP), s, d)
        ).wait_recv()

    def piece(c, dd):
        return gbuf.at[xl, seg(c * NZ + z, SUB), seg(dd, XC)]

    def c_first(c, k):
        dd = (d + k) % ND
        return remote(
            piece(c, d), piece(c, d), f1snd.at[c, k], f1rcv.at[c, d], (jnp.where(k < ND, 3, 1), t, dd)
        )

    def w_first(c, k):
        s = (d + k) % ND
        remote(piece(c, s), piece(c, s), f1snd.at[c, k], f1rcv.at[c, s], (3, t, s)).wait_recv()

    def slab(c, b, zz):
        return gbuf.at[b, seg(c * NZ + zz, SUB), :]

    def c_z(c, k):
        part = slab(c, xl, z)
        return remote(part, part, f2snd.at[c, k], f2rcv.at[c, z], (p, xl * NZ + (z + k) % NZ, d))

    def w_z(c, k):
        zz = (z + k) % NZ
        part = slab(c, xl, zz)
        remote(part, part, f2snd.at[c, k], f2rcv.at[c, zz], (p, xl * NZ + zz, d)).wait_recv()

    def c_x(c, zz):
        part = slab(c, xl, zz)
        return remote(part, part, fxsnd.at[c, zz], fxrcv.at[c, zz], (p, (1 - xl) * NZ + z, d))

    def w_x(c, zz):
        part = slab(c, 1 - xl, zz)
        remote(part, part, fxsnd.at[c, zz], fxrcv.at[c, zz], (p, (1 - xl) * NZ + z, d)).wait_recv()

    def c_core(c, b, zz):
        part = slab(c, b, zz)
        other = (p + 1 - 2 * lax.rem(p, 2), t, d)
        return remote(part, part, fcsnd.at[c, b, zz], fcrcv.at[c, b, zz], other)

    def c_one(k):
        tt = (t + k) % NT
        return remote(own, l1.at[t], l1snd.at[k], l1rcv.at[t], (p, tt, d))

    def w_one(k):
        s = (t + k) % NT
        remote(own, l1.at[s], l1snd.at[k], l1rcv.at[s], (p, s, d)).wait_recv()

    def c_two(k):
        mine = p * ND + d
        o = (mine + k) % (NP * ND)
        return remote(own2, l2.at[mine], l2snd.at[k], l2rcv.at[mine], (o // ND, t, o % ND))

    def w_two(k):
        s = (p * ND + d + k) % (NP * ND)
        remote(own2, l2.at[s], l2snd.at[k], l2rcv.at[s], (s // ND, t, s % ND)).wait_recv()

    def write(c):
        return pltpu.make_async_copy(gg.at[seg(c, ROWS), :], g_out.at[seg(c, ROWS), :], gsem.at[c])

    first, last, carrier = p == 0, p == NP - 1, lax.rem(p, 2) == 1

    load_order.start()

    @pl.when(first)
    def _():
        load_x.start()

    load_gain.start()
    for one in loads:
        one.start()

    barrier = pltpu.get_barrier_semaphore()

    def greet(dev):
        pl.semaphore_signal(barrier, inc=1, device_id=dev, device_id_type=MESH)

    loop(1, ND, lambda k: greet((p, t, (d + k) % ND)))
    loop(1, NT, lambda k: greet((p, (t + k) % NT, d)))

    @pl.when(p > 0)
    def _():
        greet((p - 1, t, d))

    @pl.when(p < NP - 1)
    def _():
        pl.semaphore_wait(barrier, ND + NT - 1)

    @pl.when(last)
    def _():
        pl.semaphore_wait(barrier, ND + NT - 2)

    load_order.wait()

    @pl.when(first)
    def _():
        load_x.wait()

        def enter(m):
            xs[m] = xin[order[m]]
            loop(1, ND, lambda k: c_in(m, k).start())
            sbuf[2 * m + d // 2, seg(d % 2, WIN), :] = xs[m, :, seg(d, DC)]

        loop(0, MB, enter)

    load_gain.wait()
    for one in loads:
        one.wait()

    offset = ((p * NT + t) * ND + d) * CH
    ids = offset + lax.broadcasted_iota(jnp.int32, (CH, ROWS), 0)
    vrows = jnp.broadcast_to(vhead[...].astype(F32).reshape(1, D), (16, D)).astype(BF)

    def up(c):
        @pl.when(first)
        def _():
            for i in range(2):
                s = 2 * (c % 2) + i

                @pl.when(s != d)
                def _():
                    w_in(c // 2, s)

        @pl.when(p > 0)
        def _():
            loop(0, NT, lambda k: w_state(c, k))

        wide = sbuf[c].astype(F32)
        square = jnp.sum(wide * wide, axis=-1, keepdims=True)
        scaled = (wide * lgain[0:1, seg(d, DC)]).astype(BF)
        usend[c, :, :FT] = jnp.dot(scaled, upw[...], preferred_element_type=F32).astype(BF)
        high = square.astype(BF).astype(F32)
        lane = lax.broadcasted_iota(jnp.int32, (ROWS, UW - FT), 1)
        usend[c, :, FT:] = jnp.where(lane < (UW - FT) // 2, high, square - high).astype(BF)
        loop(1, ND, lambda k: c_up(c, k).start())

    def hidden(c):
        total = usend[c, seg(d, SPLIT), :].astype(F32)
        for k in range(1, ND):
            w_up(c, k)
            total = total + urecv[c, (d + k) % ND].astype(F32)
        square = total[:, FT : FT + 1] + total[:, (FT + UW) // 2 : (FT + UW) // 2 + 1]
        upper = total[:, :FT] * lax.rsqrt(square / D + EPS)
        hbuf[c, seg(d, SPLIT), :] = (upper / (1.0 + jnp.exp(-upper))).astype(BF)
        loop(1, ND, lambda k: c_hid(c, k).start())

    def down(c):
        loop(1, ND, lambda k: w_hid(c, k))
        dsend[c] = jnp.dot(hbuf[c], dnw[...], preferred_element_type=F32).astype(BF)
        loop(1, NT, lambda k: c_down(c, k).start())

    def reduce(c):
        def add(k, total):
            w_down(c, k)
            return total + drecv[c, (t + k) % NT].astype(F32)

        total = lax.fori_loop(1, NT, add, tile(dsend, c, t)[...].astype(F32))
        osend[c] = (tile(sbuf, c, t)[...].astype(F32) + total).astype(BF)

        @pl.when(p < NP - 1)
        def _():
            loop(0, NT, lambda k: c_state(c, k).start())

        @pl.when(last)
        def _():
            gbuf[xl, seg(c * NZ + z, SUB), seg(d, XC)] = osend[c]
            loop(1, 2 * ND, lambda k: c_first(c, k).start())

    def along_z(c):
        @pl.when(last)
        def _():
            loop(1, ND, lambda k: w_first(c, k))

        @pl.when(p == 1)
        def _():
            loop(0, ND, lambda k: w_first(c, k))

        loop(1, NZ, lambda k: c_z(c, k).start())
        c_x(c, z).start()
        c_core(c, xl, z).start()

    def along_x(c):
        def arrived(k):
            w_z(c, k)
            zz = (z + k) % NZ
            c_x(c, zz).start()
            c_core(c, xl, zz).start()

        loop(1, NZ, arrived)

        def crossed(k):
            zz = (z + k) % NZ
            w_x(c, zz)
            c_core(c, 1 - xl, zz).start()

        loop(0, NZ, crossed)

    def head(c):
        @pl.when(jnp.logical_not(carrier))
        def _():
            loop(0, 2, lambda b: loop(0, NZ, lambda zz: c_core(c, b, zz).wait_recv()))

        rows = seg(c, ROWS)
        for i in range(2 * ND):
            b, at = i % 2, (i // 2) * XC
            cols = slice(i * XC, (i + 1) * XC)
            wide = gbuf[b, rows, at : at + XC].astype(F32)
            square = jnp.sum(wide * wide, axis=-1, keepdims=True)
            scaled = (wide * fgain[cols].reshape(1, XC)).astype(BF)
            gg[rows, cols] = scaled
            part = jnp.dot(scaled, qv[cols, :], preferred_element_type=F32)
            tpart = jnp.dot(scaled, tv[cols, :], preferred_element_type=F32)
            vpart = lax.dot_general(
                vrows[:, cols], scaled, (((1,), (1,)), ((), ())), preferred_element_type=F32
            )
            if i == 0:
                acc[...], acct[...], vacc[...], ssq[...] = part, tpart, vpart, jnp.broadcast_to(square, (ROWS, 128))
            else:
                acc[...] += part
                acct[...] += tpart
                vacc[...] += vpart
                ssq[...] += square
        write(c).start()
        factor = lax.rsqrt(ssq[...].T[0:1, :] / D + EPS)
        small = factor * D**-0.5
        logits = acc[...].T * small
        target = acct[...].T * small
        where = seg(c % 2, ROWS)
        action = acts[0:1, where] + (acts[1:2, where] - acts[0:1, where]) * order[c // 2]
        hit = ids == action
        top = jnp.max(logits, axis=0, keepdims=True)
        lt_out[:, rows] = logits
        own[0:1, rows] = top
        own[1:2, rows] = jnp.sum(jnp.exp(logits - top), axis=0, keepdims=True)
        own[2:3, rows] = jnp.sum(jnp.where(hit, logits, 0.0), axis=0, keepdims=True)
        own[3:4, rows] = jnp.sum(jnp.where(hit, target, 0.0), axis=0, keepdims=True)
        st_out[3:4, rows] = vacc[0:1, :] * small
        st_out[4:5, rows] = factor

    shift = jnp.where(last, 0, NC - 1)

    def wave(s):
        def stage(c, body, here=True):
            @pl.when((c >= 0) & (c < NC) & here)
            def _():
                body(c)

        stage(s, up)
        stage(s - 1, hidden)
        stage(s - 2, down)
        stage(s - 3, reduce)
        stage(s - 4 - shift, along_z, carrier)
        stage(s - 5 - shift, along_x, carrier)
        stage(s - 6 - shift, head)

    loop(0, 2 * NC + 5, wave)

    def combined(parts):
        top = jnp.max(parts[:, 0, :], axis=0, keepdims=True)
        total = jnp.sum(parts[:, 1, :] * jnp.exp(parts[:, 0, :] - top), axis=0, keepdims=True)
        taken = jnp.sum(parts[:, 2, :], axis=0, keepdims=True)
        target = jnp.sum(parts[:, 3, :], axis=0, keepdims=True)
        return top, total, taken, target

    loop(1, NT, lambda k: c_one(k).start())
    l1[t] = own[...]
    loop(1, NT, w_one)
    top, total, taken, target = combined(l1[...])
    own2[0:1, :] = top
    own2[1:2, :] = total
    own2[2:3, :] = taken
    own2[3:4, :] = target
    loop(1, NP * ND, lambda k: c_two(k).start())
    l2[p * ND + d] = own2[...]
    loop(1, NP * ND, w_two)
    top, total, taken, target = combined(l2[...])
    st_out[0:1, :] = top + jnp.log(total)
    st_out[1:2, :] = taken
    st_out[2:3, :] = target
    st_out[5:8, :] = jnp.zeros((3, MB * MROWS), F32)

    @pl.when(first)
    def _():
        loop(0, MB, lambda m: loop(1, ND, lambda k: c_in(m, k).wait_send()))

    def sent(c):
        loop(1, ND, lambda k: c_up(c, k).wait_send())
        loop(1, ND, lambda k: c_hid(c, k).wait_send())
        loop(1, NT, lambda k: c_down(c, k).wait_send())

        @pl.when(p < NP - 1)
        def _():
            loop(0, NT, lambda k: c_state(c, k).wait_send())

        @pl.when(last)
        def _():
            loop(1, 2 * ND, lambda k: c_first(c, k).wait_send())

        @pl.when(carrier)
        def _():
            loop(1, NZ, lambda k: c_z(c, k).wait_send())
            loop(0, NZ, lambda zz: c_x(c, zz).wait_send())
            loop(0, 2, lambda b: loop(0, NZ, lambda zz: c_core(c, b, zz).wait_send()))

        write(c).wait()

    loop(0, NC, sent)
    loop(1, NT, lambda k: c_one(k).wait_send())
    loop(1, NP * ND, lambda k: c_two(k).wait_send())


def run_trunk(order, acts, lgain, fgain, vhead, x, up, dn, q, tg):
    vm, anyw = pl.BlockSpec(memory_space=pltpu.VMEM), pl.BlockSpec(memory_space=pl.ANY)
    dma = pltpu.SemaphoreType.DMA
    rows = MB * MROWS
    return pl.pallas_call(
        trunk,
        name="trunk",
        out_shape=(
            jax.ShapeDtypeStruct((rows, D), BF),
            jax.ShapeDtypeStruct((CH, rows), F32),
            jax.ShapeDtypeStruct((8, rows), F32),
        ),
        in_specs=[anyw] * 10,
        out_specs=(anyw, vm, vm),
        scratch_shapes=[
            pltpu.SMEM((MB,), jnp.int32),
            pltpu.VMEM((MB, MROWS), jnp.int32),
            pltpu.VMEM((1, D), F32),
            pltpu.VMEM((D,), F32),
            pltpu.VMEM((D,), BF),
            pltpu.VMEM((MB, WIN, D), BF),
            pltpu.VMEM((MB, WIN, D), BF),
            pltpu.VMEM((NC, ROWS, DC), BF),
            pltpu.VMEM((DC, FT), BF),
            pltpu.VMEM((FT, DC), BF),
            pltpu.VMEM((D, CH), BF),
            pltpu.VMEM((D, CH), BF),
            pltpu.VMEM((NC, ROWS, UW), BF),
            pltpu.VMEM((NC, ND, SPLIT, UW), BF),
            pltpu.VMEM((NC, ROWS, FT), BF),
            pltpu.VMEM((NC, ROWS, DC), BF),
            pltpu.VMEM((NC, NT, SUB, XC), BF),
            pltpu.VMEM((NC, SUB, XC), BF),
            pltpu.VMEM((2, rows, ND * XC), BF),
            pltpu.VMEM((rows, D), BF),
            pltpu.VMEM((ROWS, CH), F32),
            pltpu.VMEM((ROWS, CH), F32),
            pltpu.VMEM((16, ROWS), F32),
            pltpu.VMEM((ROWS, 128), F32),
            pltpu.VMEM((4, rows), F32),
            pltpu.VMEM((NT, 4, rows), F32),
            pltpu.VMEM((4, rows), F32),
            pltpu.VMEM((NP * ND, 4, rows), F32),
            dma((10,)),
            dma((NC,)),
            dma((MB, ND)), dma((MB, ND)),
            dma((NC, ND)), dma((NC, ND)),
            dma((NC, ND)), dma((NC, ND)),
            dma((NC, NT)), dma((NC, NT)),
            dma((NC, NT)), dma((NC, NT)),
            dma((NC, 2 * ND)), dma((NC, ND)),
            dma((NC, NZ)), dma((NC, NZ)),
            dma((NC, NZ)), dma((NC, NZ)),
            dma((NC, 2, NZ)), dma((NC, 2, NZ)),
            dma((NT,)), dma((NT,)),
            dma((NP * ND,)), dma((NP * ND,)),
        ],
        compiler_params=pltpu.CompilerParams(collective_id=0, has_side_effects=True, vmem_limit_bytes=VMEM),
    )(order, acts, lgain, fgain, vhead, x, up, dn, q, tg)


FB = 512


def finish(order, rewards, done, g, lt, st, val, adv, td, vloss, qloss, grad, probs):
    @pl.when(pl.program_id(0) == 0)
    def _():
        lse, taken, target, raw, factor = (st[i : i + 1, :] for i in range(5))
        probs[...] = (jnp.exp(lt[...] - lse) * factor).T.astype(BF)
        rows = MB * MROWS

        def chosen(ref):
            a, b = ref[0:1, :], ref[1:2, :]
            return jnp.concatenate([a + (b - a) * order[m] for m in range(MB)], axis=1).astype(F32)

        reward, finished = chosen(rewards), chosen(done)
        lane = lax.broadcasted_iota(jnp.int32, (1, rows), 1)
        following = jnp.where(lane % WIN == WIN - 1, 0.0, pltpu.roll(raw, rows - 1, 1))
        error = taken - (0.5 * reward + GAMMA * (1.0 - finished) * following)
        gain = target - raw
        weight = jnp.where(gain < 0, 1.0 - TAU, TAU)
        for m in range(MB):
            cols = slice(m * MROWS, (m + 1) * MROWS)
            val[m : m + 1, :] = raw[:, cols]
            adv[m : m + 1, :] = gain[:, cols]
            td[m : m + 1, :] = error[:, cols]
        vloss[...] = jnp.sum(weight * gain * gain, axis=1, keepdims=True) / rows
        qloss[...] = jnp.sum(error * error + ALPHA * (lse - taken), axis=1, keepdims=True) / rows

    product = lax.dot_general(g[...], probs[...], (((0,), (0,)), ((), ())), preferred_element_type=F32)
    grad[...] = (product * (VQ * D**-0.5 / (MB * MROWS))).astype(BF)


def run_finish(order, rewards, done, g, lt, st):
    rows = MB * MROWS

    def whole(*shape):
        return pl.BlockSpec(shape, lambda i: (0,) * len(shape))

    small = jax.ShapeDtypeStruct((MB, MROWS), F32)
    one = jax.ShapeDtypeStruct((1, 1), F32)
    return pl.pallas_call(
        finish,
        name="finish",
        grid=(D // FB,),
        out_shape=(small, small, small, one, one, jax.ShapeDtypeStruct((D, CH), BF)),
        in_specs=[
            pl.BlockSpec(memory_space=pltpu.SMEM),
            whole(MB, MROWS),
            whole(MB, MROWS),
            pl.BlockSpec((rows, FB), lambda i: (0, i)),
            whole(CH, rows),
            whole(8, rows),
        ],
        out_specs=(
            whole(MB, MROWS),
            whole(MB, MROWS),
            whole(MB, MROWS),
            whole(1, 1),
            whole(1, 1),
            pl.BlockSpec((FB, CH), lambda i: (i, 0)),
        ),
        scratch_shapes=[pltpu.VMEM((rows, CH), BF)],
        compiler_params=pltpu.CompilerParams(vmem_limit_bytes=VMEM),
    )(order, rewards, done, g, lt, st)


def local(
    inputs, layer_gain, up_weight, down_weight, final_gain, value_head,
    q_head, target_head, actions, rewards, done, order,
):
    g, lt, st = run_trunk(
        order, actions, layer_gain, final_gain, value_head,
        inputs, up_weight, down_weight, q_head, target_head,
    )
    val, adv, td, vloss, qloss, grad = run_finish(order, rewards, done, g, lt, st)
    return val, adv, td, vloss.reshape(()), qloss.reshape(()), grad


def solution(mesh):
    in_specs = (
        P(None, "dp", None),
        P("pipe", None),
        P("pipe", "dp", "tensor"),
        P("pipe", "tensor", "dp"),
        P(),
        P(),
        P(None, ("pipe", "tensor", "dp")),
        P(None, ("pipe", "tensor", "dp")),
        P(),
        P(),
        P(),
        P(),
    )
    out_specs = (P(), P(), P(), P(), P(), P(None, ("pipe", "tensor", "dp")))
    return jax.shard_map(local, mesh=mesh, in_specs=in_specs, out_specs=out_specs, check_vma=False)
```

```python
import jax
import jax.numpy as jnp
from jax import lax
from jax.experimental import pallas as pl
from jax.experimental.pallas import tpu as pltpu
from jax.sharding import PartitionSpec as P

VQ = 65536
EPS = 1e-05
GAMMA = 0.99
TAU = 0.7
ALPHA = 0.5

MB = 2
MROWS = 256
WIN = 64
NC, ROWS = 4, 128
D = 4096
DC = 1024
FT = 896
UW = 1024
NP, NT, ND, NZ = 4, 16, 4, 8
SPLIT = 32
SUB, XC = 16, 512
QC = 256
VMEM = 63 * 2**20
CH = 256
BF, F32 = jnp.bfloat16, jnp.float32
MESH = pl.DeviceIdType.MESH


def remote(src, dst, send, recv, dev):
    return pltpu.make_async_remote_copy(
        src_ref=src, dst_ref=dst, send_sem=send, recv_sem=recv, device_id=dev, device_id_type=MESH
    )


def loop(low, high, body):
    def step(i, carry):
        body(i)
        return carry

    lax.fori_loop(low, high, step, 0)


def trunk(
    order_any, acts_any, lgain_any, fgain_any, vhead_any, x_any, up_any, dn_any, q_any, tg_any,
    g_out, lt_out, st_out,
    order, acts, lgain, fgain, vhead, xin, xs, sbuf, upw, dnw, qv, tv, usend, urecv, hbuf, dsend, drecv, osend,
    ga, gb, gt, acc, acct, vacc, ssq, own, l1, own2, l2,
    lsem, isnd, ircv, usnd, urcv, hsnd, hrcv, dsnd, drcv, ssnd, srcv,
    a1snd, a1rcv, azsnd, azrcv, axsnd, axrcv, acsnd, acrcv,
    b1snd, b1rcv, bxsnd, bxrcv, bysnd, byrcv, bcsnd, bcrcv, l1snd, l1rcv, l2snd, l2rcv,
):
    p, t, d = lax.axis_index("pipe"), lax.axis_index("tensor"), lax.axis_index("dp")
    xl, z = t // NZ, t % NZ

    def seg(i, n):
        return pl.ds(pl.multiple_of(i * n, n), n)

    loads = [
        pltpu.make_async_copy(up_any.at[0], upw, lsem.at[0]),
        pltpu.make_async_copy(dn_any.at[0], dnw, lsem.at[1]),
        pltpu.make_async_copy(q_any, qv, lsem.at[2]),
        pltpu.make_async_copy(tg_any, tv, lsem.at[3]),
        pltpu.make_async_copy(fgain_any, fgain, lsem.at[4]),
        pltpu.make_async_copy(vhead_any, vhead, lsem.at[5]),
        pltpu.make_async_copy(acts_any, acts, lsem.at[6]),
    ]
    load_x = pltpu.make_async_copy(x_any, xin, lsem.at[7])
    load_order = pltpu.make_async_copy(order_any, order, lsem.at[8])
    load_gain = pltpu.make_async_copy(lgain_any, lgain, lsem.at[9])

    def arrived(same_bytes, sem):
        pltpu.make_async_copy(same_bytes, same_bytes, sem).wait()

    def entry(m, s):
        return sbuf.at[2 * m + s // 2, seg(s % 2, WIN), :]

    def c_in(m, k):
        dd = (d + k) % ND
        return remote(xs.at[m, :, seg(dd, DC)], entry(m, d), isnd.at[0], ircv.at[m, d], (p, t, dd))

    def c_up(c, k):
        dd = (d + k) % ND
        return remote(usend.at[c, seg(dd, SPLIT), :], urecv.at[c, k], usnd.at[0], urcv.at[c], (p, t, dd))

    def c_hid(c, k):
        part = hbuf.at[c, seg(d, SPLIT), :]
        return remote(part, part, hsnd.at[0], hrcv.at[c], (p, t, (d + k) % ND))

    def tile(ref, c, tt):
        return ref.at[c, seg(tt % NZ, SUB), seg(tt // NZ, XC)]

    def c_down(c, k):
        tt = (t + k) % NT
        return remote(tile(dsend, c, tt), drecv.at[c, k], dsnd.at[0], drcv.at[c], (p, tt, d))

    def c_state(c, k):
        tt = (t + k) % NT
        return remote(osend.at[c], tile(sbuf, c, t), ssnd.at[0], srcv.at[c], (lax.rem(p + 1, NP), tt, d))

    def a_piece(c, dd):
        return ga.at[xl, seg(c * NZ + z, SUB), seg(dd, QC)]

    def c_a1(c, k):
        dev = (jnp.where(k < ND, 3, 1), t, (d + k) % ND)
        return remote(a_piece(c, d), a_piece(c, d), a1snd.at[0], a1rcv.at[c], dev)

    def a_slab(c, b, zz):
        return ga.at[b, seg(c * NZ + zz, SUB), :]

    def c_az(c, k):
        part = a_slab(c, xl, z)
        return remote(part, part, azsnd.at[0], azrcv.at[c, z], (p, xl * NZ + (z + k) % NZ, d))

    def c_ax(c, zz):
        part = a_slab(c, xl, zz)
        return remote(part, part, axsnd.at[0], axrcv.at[c, zz], (p, (1 - xl) * NZ + z, d))

    other_core = (p + 1 - 2 * lax.rem(p, 2), t, d)

    def c_ac(c, b, zz):
        part = a_slab(c, b, zz)
        return remote(part, part, acsnd.at[0], acrcv.at[c], other_core)

    def c_b1(c, k):
        part = gb.at[d, seg(c * NZ + z, SUB), seg(xl, QC)]
        dev = (jnp.where(k < NZ, 3, 1), xl * NZ + (z + k) % NZ, d)
        return remote(part, part, b1snd.at[0], b1rcv.at[c], dev)

    def b_slab(c, dd, b):
        return gb.at[dd, seg(c, ROWS), seg(b, QC)]

    def c_bx(c):
        part = b_slab(c, d, xl)
        return remote(part, part, bxsnd.at[0], bxrcv.at[c], (p, (1 - xl) * NZ + z, d))

    def c_by(c, b, k):
        part = b_slab(c, d, b)
        return remote(part, part, bysnd.at[0], byrcv.at[c, b, d], (p, t, (d + k) % ND))

    def c_bc(c, dd, b):
        part = b_slab(c, dd, b)
        return remote(part, part, bcsnd.at[0], bcrcv.at[c], other_core)

    def c_one(k):
        return remote(own, l1.at[k], l1snd.at[0], l1rcv.at[0], (p, (t + k) % NT, d))

    def c_two(k):
        o = (p * ND + d + k) % (NP * ND)
        return remote(own2, l2.at[k], l2snd.at[0], l2rcv.at[0], (o // ND, t, o % ND))

    def write(c):
        return pltpu.make_async_copy(gt.at[:, seg(c, ROWS)], g_out.at[:, seg(c, ROWS)], lsem.at[10 + c])

    first, last, carrier = p == 0, p == NP - 1, lax.rem(p, 2) == 1

    load_order.start()

    @pl.when(first)
    def _():
        load_x.start()

    load_gain.start()
    for one in loads:
        one.start()

    barrier = pltpu.get_barrier_semaphore()

    def greet(dev):
        pl.semaphore_signal(barrier, inc=1, device_id=dev, device_id_type=MESH)

    loop(1, ND, lambda k: greet((p, t, (d + k) % ND)))
    loop(1, NT, lambda k: greet((p, (t + k) % NT, d)))

    @pl.when(p > 0)
    def _():
        greet((p - 1, t, d))

    @pl.when(p < NP - 1)
    def _():
        pl.semaphore_wait(barrier, ND + NT - 1)

    @pl.when(last)
    def _():
        pl.semaphore_wait(barrier, ND + NT - 2)

    load_order.wait()

    @pl.when(first)
    def _():
        load_x.wait()

        def enter(m):
            xs[m] = xin[order[m]]
            loop(1, ND, lambda k: c_in(m, k).start())
            sbuf[2 * m + d // 2, seg(d % 2, WIN), :] = xs[m, :, seg(d, DC)]

        loop(0, MB, enter)

    load_gain.wait()
    for one in loads:
        one.wait()

    offset = ((p * NT + t) * ND + d) * CH
    ids = offset + lax.broadcasted_iota(jnp.int32, (CH, ROWS), 0)
    vrows = jnp.broadcast_to(vhead[...].astype(F32).reshape(1, D), (16, D)).astype(BF)

    def up(c):
        @pl.when(first)
        def _():
            for i in range(2):
                s = 2 * (c % 2) + i

                @pl.when(s != d)
                def _():
                    arrived(entry(c // 2, s), ircv.at[c // 2, s])

        @pl.when(p > 0)
        def _():
            arrived(sbuf.at[c], srcv.at[c])

        wide = sbuf[c].astype(F32)
        square = jnp.sum(wide * wide, axis=-1, keepdims=True)
        scaled = (wide * lgain[0:1, seg(d, DC)]).astype(BF)
        usend[c, :, :FT] = jnp.dot(scaled, upw[...], preferred_element_type=F32).astype(BF)
        high = square.astype(BF).astype(F32)
        lane = lax.broadcasted_iota(jnp.int32, (ROWS, UW - FT), 1)
        usend[c, :, FT:] = jnp.where(lane < (UW - FT) // 2, high, square - high).astype(BF)
        loop(1, ND, lambda k: c_up(c, k).start())

    def hidden(c):
        arrived(urecv.at[c, pl.ds(1, ND - 1)], urcv.at[c])
        total = usend[c, seg(d, SPLIT), :].astype(F32)
        for k in range(1, ND):
            total = total + urecv[c, k].astype(F32)
        square = total[:, FT : FT + 1] + total[:, (FT + UW) // 2 : (FT + UW) // 2 + 1]
        upper = total[:, :FT] * lax.rsqrt(square / D + EPS)
        hbuf[c, seg(d, SPLIT), :] = (upper / (1.0 + jnp.exp(-upper))).astype(BF)
        loop(1, ND, lambda k: c_hid(c, k).start())

    def down(c):
        arrived(hbuf.at[c, pl.ds(0, ROWS - SPLIT), :], hrcv.at[c])
        dsend[c] = jnp.dot(hbuf[c], dnw[...], preferred_element_type=F32).astype(BF)
        loop(1, NT, lambda k: c_down(c, k).start())

    def reduce(c):
        arrived(drecv.at[c, pl.ds(1, NT - 1)], drcv.at[c])
        total = tile(dsend, c, t)[...].astype(F32)
        for k in range(1, NT):
            total = total + drecv[c, k].astype(F32)
        osend[c] = (tile(sbuf, c, t)[...].astype(F32) + total).astype(BF)

        @pl.when(p < NP - 1)
        def _():
            loop(0, NT, lambda k: c_state(c, k).start())

        @pl.when(last)
        def _():
            at = seg(c * NZ + z, SUB)
            ga[xl, at, seg(d, QC)] = osend[c, :, :QC]
            gb[d, at, seg(xl, QC)] = osend[c, :, QC:]
            loop(1, 2 * ND, lambda k: c_a1(c, k).start())
            loop(1, 2 * NZ, lambda k: c_b1(c, k).start())

    def across(c):
        @pl.when(last)
        def _():
            arrived(drecv.at[c, pl.ds(1, ND - 1), :, pl.ds(0, QC)], a1rcv.at[c])

        @pl.when(p == 1)
        def _():
            arrived(drecv.at[c, pl.ds(0, ND), :, pl.ds(0, QC)], a1rcv.at[c])

        loop(1, NZ, lambda k: c_az(c, k).start())
        c_ax(c, z).start()
        c_ac(c, xl, z).start()

        @pl.when(last)
        def _():
            arrived(drecv.at[c, pl.ds(1, NZ - 1), :, pl.ds(0, QC)], b1rcv.at[c])

        @pl.when(p == 1)
        def _():
            arrived(drecv.at[c, pl.ds(0, NZ), :, pl.ds(0, QC)], b1rcv.at[c])

        c_bx(c).start()
        loop(1, ND, lambda k: c_by(c, xl, k).start())
        c_bc(c, d, xl).start()

    def onward(c):
        def a_come(k):
            zz = (z + k) % NZ
            arrived(a_slab(c, xl, zz), azrcv.at[c, zz])
            c_ax(c, zz).start()
            c_ac(c, xl, zz).start()

        arrived(b_slab(c, d, 1 - xl), bxrcv.at[c])
        loop(1, ND, lambda k: c_by(c, 1 - xl, k).start())
        c_bc(c, d, 1 - xl).start()
        loop(1, NZ, a_come)

        def a_crossed(k):
            zz = (z + k) % NZ
            arrived(a_slab(c, 1 - xl, zz), axrcv.at[c, zz])
            c_ac(c, 1 - xl, zz).start()

        loop(0, NZ, a_crossed)

        def b_come(i):
            b, dd = (xl + i // ND) % 2, (d + i % ND) % ND

            @pl.when(dd != d)
            def _():
                arrived(b_slab(c, dd, b), byrcv.at[c, b, dd])
                c_bc(c, dd, b).start()

        loop(0, 2 * ND, b_come)

    def head(c):
        @pl.when(jnp.logical_not(carrier))
        def _():
            arrived(ga.at[:, seg(c, ROWS), :], acrcv.at[c])
            arrived(gb.at[:, seg(c, ROWS), :], bcrcv.at[c])

        rows = seg(c, ROWS)
        for i in range(2 * ND):
            b, dd = i % 2, i // 2
            cols = slice(i * XC, (i + 1) * XC)
            wide = jnp.concatenate(
                [ga[b, rows, dd * QC : (dd + 1) * QC], gb[dd, rows, b * QC : (b + 1) * QC]], axis=1
            ).astype(F32)
            square = jnp.sum(wide * wide, axis=-1, keepdims=True)
            scaled = (wide * fgain[cols].reshape(1, XC)).astype(BF)
            gt[cols, rows] = scaled.T
            part = jnp.dot(scaled, qv[cols, :], preferred_element_type=F32)
            tpart = jnp.dot(scaled, tv[cols, :], preferred_element_type=F32)
            vpart = lax.dot_general(
                vrows[:, cols], scaled, (((1,), (1,)), ((), ())), preferred_element_type=F32
            )
            if i == 0:
                acc[...], acct[...], vacc[...], ssq[...] = part, tpart, vpart, jnp.broadcast_to(square, (ROWS, 128))
            else:
                acc[...] += part
                acct[...] += tpart
                vacc[...] += vpart
                ssq[...] += square
        write(c).start()
        factor = lax.rsqrt(ssq[...].T[0:1, :] / D + EPS)
        small = factor * D**-0.5
        logits = acc[...].T * small
        target = acct[...].T * small
        where = seg(c % 2, ROWS)
        action = acts[0:1, where] + (acts[1:2, where] - acts[0:1, where]) * order[c // 2]
        hit = ids == action
        top = jnp.max(logits, axis=0, keepdims=True)
        lt_out[:, rows] = logits
        own[0:1, rows] = top + jnp.log(jnp.sum(jnp.exp(logits - top), axis=0, keepdims=True))
        own[1:2, rows] = jnp.sum(jnp.where(hit, logits, 0.0), axis=0, keepdims=True)
        own[2:3, rows] = jnp.sum(jnp.where(hit, target, 0.0), axis=0, keepdims=True)
        own[3:4, rows] = jnp.zeros((1, ROWS), F32)
        st_out[3:4, rows] = vacc[0:1, :] * small
        st_out[4:5, rows] = factor

    shift = jnp.where(last, 0, NC - 1)

    def wave(s):
        def stage(c, body, here=True):
            @pl.when((c >= 0) & (c < NC) & here)
            def _():
                body(c)

        stage(s, up)
        stage(s - 1, hidden)
        stage(s - 2, down)
        stage(s - 3, reduce)
        stage(s - 4 - shift, across, carrier)
        stage(s - 6 - shift, head)
        stage(s - 5 - shift, onward, carrier)

    loop(0, 2 * NC + 5, wave)

    def combined(parts):
        top = jnp.max(parts, axis=0)
        merged = top + jnp.log(jnp.sum(jnp.exp(parts - top[None]), axis=0))
        row = lax.broadcasted_iota(jnp.int32, top.shape, 0)
        return jnp.where(row == 0, merged, jnp.sum(parts, axis=0))

    loop(1, NT, lambda k: c_one(k).start())
    l1[0] = own[...]
    arrived(l1.at[pl.ds(1, NT - 1)], l1rcv.at[0])
    own2[...] = combined(l1[...])
    loop(1, NP * ND, lambda k: c_two(k).start())
    l2[0] = own2[...]
    arrived(l2.at[pl.ds(1, NP * ND - 1)], l2rcv.at[0])
    everywhere = combined(l2[...])
    st_out[0:3, :] = everywhere[0:3, :]
    st_out[5:8, :] = jnp.zeros((3, MB * MROWS), F32)

    @pl.when(first)
    def _():
        arrived(xs.at[:, :, pl.ds(0, (ND - 1) * DC)], isnd.at[0])

    arrived(urecv.at[:, pl.ds(1, ND - 1)], usnd.at[0])
    arrived(hbuf.at[:, pl.ds(0, ROWS - SPLIT), :], hsnd.at[0])
    arrived(drecv.at[:, pl.ds(1, NT - 1)], dsnd.at[0])

    @pl.when(p < NP - 1)
    def _():
        arrived(drecv, ssnd.at[0])

    @pl.when(last)
    def _():
        arrived(drecv.at[:, pl.ds(1, 2 * ND - 1), :, pl.ds(0, QC)], a1snd.at[0])
        arrived(drecv.at[:, pl.ds(1, 2 * NZ - 1), :, pl.ds(0, QC)], b1snd.at[0])

    @pl.when(carrier)
    def _():
        arrived(ga.at[0, pl.ds(0, NC * (NZ - 1) * SUB), :], azsnd.at[0])
        arrived(ga.at[0], axsnd.at[0])
        arrived(ga, acsnd.at[0])
        arrived(gb.at[0, :, pl.ds(0, QC)], bxsnd.at[0])
        arrived(gb.at[pl.ds(1, ND - 1)], bysnd.at[0])
        arrived(gb, bcsnd.at[0])

    loop(0, NC, lambda c: write(c).wait())
    arrived(l1.at[pl.ds(1, NT - 1)], l1snd.at[0])
    arrived(l2.at[pl.ds(1, NP * ND - 1)], l2snd.at[0])


def run_trunk(order, acts, lgain, fgain, vhead, x, up, dn, q, tg):
    vm, anyw = pl.BlockSpec(memory_space=pltpu.VMEM), pl.BlockSpec(memory_space=pl.ANY)
    dma = pltpu.SemaphoreType.DMA
    rows = MB * MROWS
    return pl.pallas_call(
        trunk,
        name="trunk",
        out_shape=(
            jax.ShapeDtypeStruct((D, rows), BF),
            jax.ShapeDtypeStruct((CH, rows), F32),
            jax.ShapeDtypeStruct((8, rows), F32),
        ),
        in_specs=[anyw] * 10,
        out_specs=(anyw, vm, vm),
        scratch_shapes=[
            pltpu.SMEM((MB,), jnp.int32),
            pltpu.VMEM((MB, MROWS), jnp.int32),
            pltpu.VMEM((1, D), F32),
            pltpu.VMEM((D,), F32),
            pltpu.VMEM((D,), BF),
            pltpu.VMEM((MB, WIN, D), BF),
            pltpu.VMEM((MB, WIN, D), BF),
            pltpu.VMEM((NC, ROWS, DC), BF),
            pltpu.VMEM((DC, FT), BF),
            pltpu.VMEM((FT, DC), BF),
            pltpu.VMEM((D, CH), BF),
            pltpu.VMEM((D, CH), BF),
            pltpu.VMEM((NC, ROWS, UW), BF),
            pltpu.VMEM((NC, ND, SPLIT, UW), BF),
            pltpu.VMEM((NC, ROWS, FT), BF),
            pltpu.VMEM((NC, ROWS, DC), BF),
            pltpu.VMEM((NC, NT, SUB, XC), BF),
            pltpu.VMEM((NC, SUB, XC), BF),
            pltpu.VMEM((2, rows, ND * QC), BF),
            pltpu.VMEM((ND, rows, 2 * QC), BF),
            pltpu.VMEM((D, rows), BF),
            pltpu.VMEM((ROWS, CH), F32),
            pltpu.VMEM((ROWS, CH), F32),
            pltpu.VMEM((16, ROWS), F32),
            pltpu.VMEM((ROWS, 128), F32),
            pltpu.VMEM((4, rows), F32),
            pltpu.VMEM((NT, 4, rows), F32),
            pltpu.VMEM((4, rows), F32),
            pltpu.VMEM((NP * ND, 4, rows), F32),
            dma((10 + NC,)),
            dma((1,)), dma((MB, ND)),
            dma((1,)), dma((NC,)),
            dma((1,)), dma((NC,)),
            dma((1,)), dma((NC,)),
            dma((1,)), dma((NC,)),
            dma((1,)), dma((NC,)),
            dma((1,)), dma((NC, NZ)),
            dma((1,)), dma((NC, NZ)),
            dma((1,)), dma((NC,)),
            dma((1,)), dma((NC,)),
            dma((1,)), dma((NC,)),
            dma((1,)), dma((NC, 2, ND)),
            dma((1,)), dma((NC,)),
            dma((1,)), dma((1,)),
            dma((1,)), dma((1,)),
        ],
        compiler_params=pltpu.CompilerParams(collective_id=0, has_side_effects=True, vmem_limit_bytes=VMEM),
    )(order, acts, lgain, fgain, vhead, x, up, dn, q, tg)


FB = 512


def finish(order, rewards, done, g, lt, st, val, adv, td, vloss, qloss, grad, probs):
    @pl.when(pl.program_id(0) == 0)
    def _():
        lse, taken, target, raw, factor = (st[i : i + 1, :] for i in range(5))
        probs[...] = (jnp.exp(lt[...] - lse) * factor).astype(BF)
        rows = MB * MROWS

        def chosen(ref):
            a, b = ref[0:1, :], ref[1:2, :]
            return jnp.concatenate([a + (b - a) * order[m] for m in range(MB)], axis=1).astype(F32)

        reward, finished = chosen(rewards), chosen(done)
        lane = lax.broadcasted_iota(jnp.int32, (1, rows), 1)
        following = jnp.where(lane % WIN == WIN - 1, 0.0, pltpu.roll(raw, rows - 1, 1))
        error = taken - (0.5 * reward + GAMMA * (1.0 - finished) * following)
        gain = target - raw
        weight = jnp.where(gain < 0, 1.0 - TAU, TAU)
        for m in range(MB):
            cols = slice(m * MROWS, (m + 1) * MROWS)
            val[m : m + 1, :] = raw[:, cols]
            adv[m : m + 1, :] = gain[:, cols]
            td[m : m + 1, :] = error[:, cols]
        vloss[...] = jnp.sum(weight * gain * gain, axis=1, keepdims=True) / rows
        qloss[...] = jnp.sum(error * error + ALPHA * (lse - taken), axis=1, keepdims=True) / rows

    product = lax.dot_general(g[...], probs[...], (((1,), (1,)), ((), ())), preferred_element_type=F32)
    grad[...] = (product * (VQ * D**-0.5 / (MB * MROWS))).astype(BF)


def run_finish(order, rewards, done, g, lt, st):
    rows = MB * MROWS

    def whole(*shape):
        return pl.BlockSpec(shape, lambda i: (0,) * len(shape))

    small = jax.ShapeDtypeStruct((MB, MROWS), F32)
    one = jax.ShapeDtypeStruct((1, 1), F32)
    return pl.pallas_call(
        finish,
        name="finish",
        grid=(D // FB,),
        out_shape=(small, small, small, one, one, jax.ShapeDtypeStruct((D, CH), BF)),
        in_specs=[
            pl.BlockSpec(memory_space=pltpu.SMEM),
            whole(MB, MROWS),
            whole(MB, MROWS),
            pl.BlockSpec((FB, rows), lambda i: (i, 0)),
            whole(CH, rows),
            whole(8, rows),
        ],
        out_specs=(
            whole(MB, MROWS),
            whole(MB, MROWS),
            whole(MB, MROWS),
            whole(1, 1),
            whole(1, 1),
            pl.BlockSpec((FB, CH), lambda i: (i, 0)),
        ),
        scratch_shapes=[pltpu.VMEM((CH, rows), BF)],
        compiler_params=pltpu.CompilerParams(vmem_limit_bytes=VMEM),
    )(order, rewards, done, g, lt, st)


def local(
    inputs, layer_gain, up_weight, down_weight, final_gain, value_head,
    q_head, target_head, actions, rewards, done, order,
):
    g, lt, st = run_trunk(
        order, actions, layer_gain, final_gain, value_head,
        inputs, up_weight, down_weight, q_head, target_head,
    )
    val, adv, td, vloss, qloss, grad = run_finish(order, rewards, done, g, lt, st)
    return val, adv, td, vloss.reshape(()), qloss.reshape(()), grad


def solution(mesh):
    in_specs = (
        P(None, "dp", None),
        P("pipe", None),
        P("pipe", "dp", "tensor"),
        P("pipe", "tensor", "dp"),
        P(),
        P(),
        P(None, ("pipe", "tensor", "dp")),
        P(None, ("pipe", "tensor", "dp")),
        P(),
        P(),
        P(),
        P(),
    )
    out_specs = (P(), P(), P(), P(), P(), P(None, ("pipe", "tensor", "dp")))
    return jax.shard_map(local, mesh=mesh, in_specs=in_specs, out_specs=out_specs, check_vma=False)
```

```python
import jax
import jax.numpy as jnp
from jax import lax
from jax.experimental import pallas as pl
from jax.experimental.pallas import tpu as pltpu
from jax.sharding import PartitionSpec as P

VQ = 65536
EPS = 1e-05
GAMMA = 0.99
TAU = 0.7
ALPHA = 0.5

MB = 2
MROWS = 256
WIN = 64
NC, ROWS = 4, 128
D = 4096
DC = 1024
FT = 896
UW = 1024
NP, NT, ND, NZ = 4, 16, 4, 8
SPLIT = 32
SUB, XC = 16, 512
QC = 256
VMEM = 63 * 2**20
CH = 256
BF, F32 = jnp.bfloat16, jnp.float32
MESH = pl.DeviceIdType.MESH


def remote(src, dst, send, recv, dev):
    return pltpu.make_async_remote_copy(
        src_ref=src, dst_ref=dst, send_sem=send, recv_sem=recv, device_id=dev, device_id_type=MESH
    )


def loop(low, high, body):
    def step(i, carry):
        body(i)
        return carry

    lax.fori_loop(low, high, step, 0)


def trunk(
    order_any, acts_any, lgain_any, fgain_any, vhead_any, x_any, up_any, dn_any, q_any, tg_any,
    g_out, lt_out, st_out,
    order, acts, lgain, fgain, vhead, xin, xs, sbuf, upw, dnw, qv, tv, usend, urecv, hbuf, dsend, drecv, osend,
    ga, gb, gt, acc, acct, vacc, ssq, own, l1, own2, l2,
    lsem, isnd, ircv, usnd, urcv, hsnd, hrcv, dsnd, drcv, ssnd, srcv,
    a1snd, a1rcv, azsnd, azrcv, axsnd, axrcv, acsnd, acrcv,
    b1snd, b1rcv, bxsnd, bxrcv, bysnd, byrcv, bcsnd, bcrcv, l1snd, l1rcv, l2snd, l2rcv,
):
    p, t, d = lax.axis_index("pipe"), lax.axis_index("tensor"), lax.axis_index("dp")
    xl, z = t // NZ, t % NZ

    def seg(i, n):
        return pl.ds(pl.multiple_of(i * n, n), n)

    loads = [
        pltpu.make_async_copy(up_any.at[0], upw, lsem.at[0]),
        pltpu.make_async_copy(dn_any.at[0], dnw, lsem.at[1]),
        pltpu.make_async_copy(q_any, qv, lsem.at[2]),
        pltpu.make_async_copy(tg_any, tv, lsem.at[3]),
        pltpu.make_async_copy(fgain_any, fgain, lsem.at[4]),
        pltpu.make_async_copy(vhead_any, vhead, lsem.at[5]),
        pltpu.make_async_copy(acts_any, acts, lsem.at[6]),
    ]
    load_x = pltpu.make_async_copy(x_any, xin, lsem.at[7])
    load_order = pltpu.make_async_copy(order_any, order, lsem.at[8])
    load_gain = pltpu.make_async_copy(lgain_any, lgain, lsem.at[9])

    def arrived(same_bytes, sem):
        pltpu.make_async_copy(same_bytes, same_bytes, sem).wait()

    def entry(m, s):
        return sbuf.at[2 * m + s // 2, seg(s % 2, WIN), :]

    def c_in(m, k):
        dd = (d + k) % ND
        return remote(xs.at[m, :, seg(dd, DC)], entry(m, d), isnd.at[0], ircv.at[m, d], (p, t, dd))

    def c_up(c, k):
        dd = (d + k) % ND
        return remote(usend.at[c, seg(dd, SPLIT), :], urecv.at[c, k], usnd.at[0], urcv.at[c], (p, t, dd))

    def c_hid(c, k):
        part = hbuf.at[c, seg(d, SPLIT), :]
        return remote(part, part, hsnd.at[0], hrcv.at[c], (p, t, (d + k) % ND))

    def tile(ref, c, tt):
        return ref.at[c, seg(tt % NZ, SUB), seg(tt // NZ, XC)]

    def peer(i):
        j = i // 2
        away = (NZ // 2 + jnp.where(j % 2 == 1, -((j + 1) // 2), j // 2)) % NZ
        return (xl + 1 + i % 2) % 2 * NZ + (z + away) % NZ

    def c_down(c, k):
        tt = peer(k)
        return remote(tile(dsend, c, tt), drecv.at[c, k], dsnd.at[0], drcv.at[c], (p, tt, d))

    def c_state(c, k):
        return remote(osend.at[c], tile(sbuf, c, t), ssnd.at[0], srcv.at[c], (lax.rem(p + 1, NP), peer(k), d))

    def a_piece(c, dd):
        return ga.at[xl, seg(c * NZ + z, SUB), seg(dd, QC)]

    def c_a1(c, k):
        dev = (jnp.where(k < ND, 3, 1), t, (d + k) % ND)
        return remote(a_piece(c, d), a_piece(c, d), a1snd.at[0], a1rcv.at[c], dev)

    def a_slab(c, b, zz):
        return ga.at[b, seg(c * NZ + zz, SUB), :]

    def c_az(c, k):
        part = a_slab(c, xl, z)
        return remote(part, part, azsnd.at[0], azrcv.at[c, z], (p, xl * NZ + (z + k) % NZ, d))

    def c_ax(c, zz):
        part = a_slab(c, xl, zz)
        return remote(part, part, axsnd.at[0], axrcv.at[c, zz], (p, (1 - xl) * NZ + z, d))

    other_core = (p + 1 - 2 * lax.rem(p, 2), t, d)

    def c_ac(c, b, zz):
        part = a_slab(c, b, zz)
        return remote(part, part, acsnd.at[0], acrcv.at[c], other_core)

    def c_b1(c, k):
        dev = (jnp.where(k < NZ, 2, 0), xl * NZ + (z + k) % NZ, d)
        src, dst = osend.at[c, :, pl.ds(QC, QC)], gb.at[d, seg(c * NZ + z, SUB), seg(xl, QC)]
        return remote(src, dst, b1snd.at[0], b1rcv.at[c], dev)

    def b_slab(c, dd, b):
        return gb.at[dd, seg(c, ROWS), seg(b, QC)]

    def c_bx(c):
        part = b_slab(c, d, xl)
        return remote(part, part, bxsnd.at[0], bxrcv.at[c], (p, (1 - xl) * NZ + z, d))

    def c_by(c, b, k):
        part = b_slab(c, d, b)
        return remote(part, part, bysnd.at[0], byrcv.at[c, b, d], (p, t, (d + k) % ND))

    def c_bc(c, dd, b):
        part = b_slab(c, dd, b)
        return remote(part, part, bcsnd.at[0], bcrcv.at[c], other_core)

    def c_one(k):
        return remote(own, l1.at[k], l1snd.at[0], l1rcv.at[0], (p, peer(k), d))

    def c_two(k):
        o = (p * ND + d + k) % (NP * ND)
        return remote(own2, l2.at[k], l2snd.at[0], l2rcv.at[0], (o // ND, t, o % ND))

    def write(c):
        return pltpu.make_async_copy(gt.at[:, seg(c, ROWS)], g_out.at[:, seg(c, ROWS)], lsem.at[10 + c])

    first, last, even, odd = p == 0, p == NP - 1, lax.rem(p, 2) == 0, lax.rem(p, 2) == 1

    load_order.start()

    @pl.when(first)
    def _():
        load_x.start()

    load_gain.start()
    for one in loads:
        one.start()

    barrier = pltpu.get_barrier_semaphore()

    def greet(dev):
        pl.semaphore_signal(barrier, inc=1, device_id=dev, device_id_type=MESH)

    loop(1, ND, lambda k: greet((p, t, (d + k) % ND)))
    loop(1, NT, lambda k: greet((p, (t + k) % NT, d)))

    @pl.when(p > 0)
    def _():
        greet((p - 1, t, d))

    @pl.when(p < NP - 1)
    def _():
        pl.semaphore_wait(barrier, ND + NT - 1)

    @pl.when(last)
    def _():
        pl.semaphore_wait(barrier, ND + NT - 2)

    load_order.wait()

    @pl.when(first)
    def _():
        load_x.wait()

        def enter(m):
            xs[m] = xin[order[m]]
            loop(1, ND, lambda k: c_in(m, k).start())
            sbuf[2 * m + d // 2, seg(d % 2, WIN), :] = xs[m, :, seg(d, DC)]

        loop(0, MB, enter)

    load_gain.wait()
    for one in loads:
        one.wait()

    offset = ((p * NT + t) * ND + d) * CH
    ids = offset + lax.broadcasted_iota(jnp.int32, (CH, ROWS), 0)
    vrow = vhead[...].astype(F32).reshape(1, D)

    def up(c):
        @pl.when(first)
        def _():
            for i in range(2):
                s = 2 * (c % 2) + i

                @pl.when(s != d)
                def _():
                    arrived(entry(c // 2, s), ircv.at[c // 2, s])

        @pl.when(p > 0)
        def _():
            arrived(sbuf.at[c], srcv.at[c])

        wide = sbuf[c].astype(F32)
        square = jnp.sum(wide * wide, axis=-1, keepdims=True)
        scaled = (wide * lgain[0:1, seg(d, DC)]).astype(BF)
        usend[c, :, :FT] = jnp.dot(scaled, upw[...], preferred_element_type=F32).astype(BF)
        high = square.astype(BF).astype(F32)
        lane = lax.broadcasted_iota(jnp.int32, (ROWS, UW - FT), 1)
        usend[c, :, FT:] = jnp.where(lane < (UW - FT) // 2, high, square - high).astype(BF)
        loop(1, ND, lambda k: c_up(c, k).start())

    def hidden(c):
        arrived(urecv.at[c, pl.ds(1, ND - 1)], urcv.at[c])
        total = usend[c, seg(d, SPLIT), :].astype(F32)
        for k in range(1, ND):
            total = total + urecv[c, k].astype(F32)
        square = total[:, FT : FT + 1] + total[:, (FT + UW) // 2 : (FT + UW) // 2 + 1]
        upper = total[:, :FT] * lax.rsqrt(square / D + EPS)
        hbuf[c, seg(d, SPLIT), :] = (upper / (1.0 + jnp.exp(-upper))).astype(BF)
        loop(1, ND, lambda k: c_hid(c, k).start())

    def down(c):
        arrived(hbuf.at[c, pl.ds(0, ROWS - SPLIT), :], hrcv.at[c])
        dsend[c] = jnp.dot(hbuf[c], dnw[...], preferred_element_type=F32).astype(BF)
        loop(0, NT - 1, lambda k: c_down(c, k).start())

    def reduce(c):
        arrived(drecv.at[c, pl.ds(0, NT - 1)], drcv.at[c])
        total = tile(dsend, c, t)[...].astype(F32)
        for k in range(NT - 1):
            total = total + drecv[c, k].astype(F32)
        osend[c] = (tile(sbuf, c, t)[...].astype(F32) + total).astype(BF)

        @pl.when(p < NP - 1)
        def _():
            loop(0, NT, lambda k: c_state(c, k).start())

        @pl.when(last)
        def _():
            at = seg(c * NZ + z, SUB)
            ga[xl, at, seg(d, QC)] = osend[c, :, :QC]
            loop(1, 2 * ND, lambda k: c_a1(c, k).start())
            loop(0, 2 * NZ, lambda k: c_b1(c, k).start())

    def a_across(c):
        @pl.when(last)
        def _():
            arrived(drecv.at[c, pl.ds(1, ND - 1), :, pl.ds(0, QC)], a1rcv.at[c])

        @pl.when(p == 1)
        def _():
            arrived(drecv.at[c, pl.ds(0, ND), :, pl.ds(0, QC)], a1rcv.at[c])

        loop(1, NZ, lambda k: c_az(c, k).start())
        c_ax(c, z).start()
        c_ac(c, xl, z).start()

    def a_onward(c):
        def come(k):
            zz = (z + k) % NZ
            arrived(a_slab(c, xl, zz), azrcv.at[c, zz])
            c_ax(c, zz).start()
            c_ac(c, xl, zz).start()

        loop(1, NZ, come)

    def a_landing(c):
        def crossed(k):
            zz = (z + k) % NZ
            arrived(a_slab(c, 1 - xl, zz), axrcv.at[c, zz])
            c_ac(c, 1 - xl, zz).start()

        loop(0, NZ, crossed)

    def b_across(c):
        arrived(drecv.at[c, pl.ds(0, NZ), :, pl.ds(0, QC)], b1rcv.at[c])
        c_bx(c).start()
        loop(1, ND, lambda k: c_by(c, xl, k).start())
        c_bc(c, d, xl).start()

    def b_onward(c):
        arrived(b_slab(c, d, 1 - xl), bxrcv.at[c])
        loop(1, ND, lambda k: c_by(c, 1 - xl, k).start())
        c_bc(c, d, 1 - xl).start()

    def b_landing(c):
        def come(b, k):
            dd = (d + k) % ND
            arrived(b_slab(c, dd, b), byrcv.at[c, b, dd])
            c_bc(c, dd, b).start()

        loop(1, ND, lambda k: come(xl, k))
        loop(1, ND, lambda k: come(1 - xl, k))

    def folded(block):
        return sum(block[:, i * 128 : (i + 1) * 128] for i in range(XC // 128))

    def head(c):
        @pl.when(even)
        def _():
            arrived(ga.at[:, seg(c, ROWS), :], acrcv.at[c])

        @pl.when(odd)
        def _():
            arrived(gb.at[:, seg(c, ROWS), :], bcrcv.at[c])

        rows = seg(c, ROWS)
        for i in range(2 * ND):
            b, dd = i % 2, i // 2
            cols = slice(i * XC, (i + 1) * XC)
            wide = jnp.concatenate(
                [ga[b, rows, dd * QC : (dd + 1) * QC], gb[dd, rows, b * QC : (b + 1) * QC]], axis=1
            ).astype(F32)
            scaled = (wide * fgain[cols].reshape(1, XC)).astype(BF)
            gt[cols, rows] = scaled.T
            part = jnp.dot(scaled, qv[cols, :], preferred_element_type=F32)
            tpart = jnp.dot(scaled, tv[cols, :], preferred_element_type=F32)
            vpart = folded(scaled.astype(F32) * vrow[:, cols])
            square = folded(wide * wide)
            if i == 0:
                acc[...], acct[...], vacc[...], ssq[...] = part, tpart, vpart, square
            else:
                acc[...] += part
                acct[...] += tpart
                vacc[...] += vpart
                ssq[...] += square
        write(c).start()
        factor = lax.rsqrt(jnp.sum(ssq[...].T, axis=0, keepdims=True) / D + EPS)
        small = factor * D**-0.5
        logits = acc[...].T * small
        target = acct[...].T * small
        where = seg(c % 2, ROWS)
        action = acts[0:1, where] + (acts[1:2, where] - acts[0:1, where]) * order[c // 2]
        hit = ids == action
        top = jnp.max(logits, axis=0, keepdims=True)
        lt_out[:, rows] = logits
        own[0:1, rows] = top + jnp.log(jnp.sum(jnp.exp(logits - top), axis=0, keepdims=True))
        own[1:2, rows] = jnp.sum(jnp.where(hit, logits, 0.0), axis=0, keepdims=True)
        own[2:3, rows] = jnp.sum(jnp.where(hit, target, 0.0), axis=0, keepdims=True)
        own[3:4, rows] = jnp.zeros((1, ROWS), F32)
        st_out[3:4, rows] = jnp.sum(vacc[...].T, axis=0, keepdims=True) * small
        st_out[4:5, rows] = factor

    shift = jnp.where(last, 0, 2)

    def wave(s):
        def stage(c, body, here=True):
            @pl.when((c >= 0) & (c < NC) & here)
            def _():
                body(c)

        stage(s - 2, hidden)
        stage(s - 3, down)
        stage(s - 5, reduce)
        stage(s, up)
        stage(s - 8 - shift, a_onward, odd)
        stage(s - 9 - shift, a_landing, odd)
        stage(s - 6 - shift, a_across, odd)
        stage(s - 6 - shift, b_across, even)
        stage(s - 7 - shift, b_onward, even)
        stage(s - 8 - shift, b_landing, even)
        stage(s - 10 - shift, head)

    loop(0, NC + 12, wave)

    def combined(parts):
        top = jnp.max(parts, axis=0)
        merged = top + jnp.log(jnp.sum(jnp.exp(parts - top[None]), axis=0))
        row = lax.broadcasted_iota(jnp.int32, top.shape, 0)
        return jnp.where(row == 0, merged, jnp.sum(parts, axis=0))

    loop(0, NT - 1, lambda k: c_one(k).start())
    l1[NT - 1] = own[...]
    arrived(l1.at[pl.ds(0, NT - 1)], l1rcv.at[0])
    own2[...] = combined(l1[...])
    loop(1, NP * ND, lambda k: c_two(k).start())
    l2[0] = own2[...]
    arrived(l2.at[pl.ds(1, NP * ND - 1)], l2rcv.at[0])
    everywhere = combined(l2[...])
    st_out[0:3, :] = everywhere[0:3, :]
    st_out[5:8, :] = jnp.zeros((3, MB * MROWS), F32)

    @pl.when(first)
    def _():
        arrived(xs.at[:, :, pl.ds(0, (ND - 1) * DC)], isnd.at[0])

    arrived(urecv.at[:, pl.ds(1, ND - 1)], usnd.at[0])
    arrived(hbuf.at[:, pl.ds(0, ROWS - SPLIT), :], hsnd.at[0])
    arrived(drecv.at[:, pl.ds(1, NT - 1)], dsnd.at[0])

    @pl.when(p < NP - 1)
    def _():
        arrived(drecv, ssnd.at[0])

    @pl.when(last)
    def _():
        arrived(drecv.at[:, pl.ds(1, 2 * ND - 1), :, pl.ds(0, QC)], a1snd.at[0])
        arrived(drecv.at[:, :, :, pl.ds(0, QC)], b1snd.at[0])

    @pl.when(odd)
    def _():
        arrived(ga.at[0, pl.ds(0, NC * (NZ - 1) * SUB), :], azsnd.at[0])
        arrived(ga.at[0], axsnd.at[0])
        arrived(ga, acsnd.at[0])

    @pl.when(even)
    def _():
        arrived(gb.at[0, :, pl.ds(0, QC)], bxsnd.at[0])
        arrived(gb.at[pl.ds(1, ND - 1)], bysnd.at[0])
        arrived(gb, bcsnd.at[0])

    loop(0, NC, lambda c: write(c).wait())
    arrived(l1.at[pl.ds(1, NT - 1)], l1snd.at[0])
    arrived(l2.at[pl.ds(1, NP * ND - 1)], l2snd.at[0])


def run_trunk(order, acts, lgain, fgain, vhead, x, up, dn, q, tg):
    vm, anyw = pl.BlockSpec(memory_space=pltpu.VMEM), pl.BlockSpec(memory_space=pl.ANY)
    dma = pltpu.SemaphoreType.DMA
    rows = MB * MROWS
    return pl.pallas_call(
        trunk,
        name="trunk",
        out_shape=(
            jax.ShapeDtypeStruct((D, rows), BF),
            jax.ShapeDtypeStruct((CH, rows), F32),
            jax.ShapeDtypeStruct((8, rows), F32),
        ),
        in_specs=[anyw] * 10,
        out_specs=(anyw, vm, vm),
        scratch_shapes=[
            pltpu.SMEM((MB,), jnp.int32),
            pltpu.VMEM((MB, MROWS), jnp.int32),
            pltpu.VMEM((1, D), F32),
            pltpu.VMEM((D,), F32),
            pltpu.VMEM((D,), BF),
            pltpu.VMEM((MB, WIN, D), BF),
            pltpu.VMEM((MB, WIN, D), BF),
            pltpu.VMEM((NC, ROWS, DC), BF),
            pltpu.VMEM((DC, FT), BF),
            pltpu.VMEM((FT, DC), BF),
            pltpu.VMEM((D, CH), BF),
            pltpu.VMEM((D, CH), BF),
            pltpu.VMEM((NC, ROWS, UW), BF),
            pltpu.VMEM((NC, ND, SPLIT, UW), BF),
            pltpu.VMEM((NC, ROWS, FT), BF),
            pltpu.VMEM((NC, ROWS, DC), BF),
            pltpu.VMEM((NC, NT, SUB, XC), BF),
            pltpu.VMEM((NC, SUB, XC), BF),
            pltpu.VMEM((2, rows, ND * QC), BF),
            pltpu.VMEM((ND, rows, 2 * QC), BF),
            pltpu.VMEM((D, rows), BF),
            pltpu.VMEM((ROWS, CH), F32),
            pltpu.VMEM((ROWS, CH), F32),
            pltpu.VMEM((ROWS, 128), F32),
            pltpu.VMEM((ROWS, 128), F32),
            pltpu.VMEM((4, rows), F32),
            pltpu.VMEM((NT, 4, rows), F32),
            pltpu.VMEM((4, rows), F32),
            pltpu.VMEM((NP * ND, 4, rows), F32),
            dma((10 + NC,)),
            dma((1,)), dma((MB, ND)),
            dma((1,)), dma((NC,)),
            dma((1,)), dma((NC,)),
            dma((1,)), dma((NC,)),
            dma((1,)), dma((NC,)),
            dma((1,)), dma((NC,)),
            dma((1,)), dma((NC, NZ)),
            dma((1,)), dma((NC, NZ)),
            dma((1,)), dma((NC,)),
            dma((1,)), dma((NC,)),
            dma((1,)), dma((NC,)),
            dma((1,)), dma((NC, 2, ND)),
            dma((1,)), dma((NC,)),
            dma((1,)), dma((1,)),
            dma((1,)), dma((1,)),
        ],
        compiler_params=pltpu.CompilerParams(collective_id=0, has_side_effects=True, vmem_limit_bytes=VMEM),
    )(order, acts, lgain, fgain, vhead, x, up, dn, q, tg)


FB = 2048


def finish(order, rewards, done, g, lt, st, val, adv, td, vloss, qloss, grad, probs):
    @pl.when(pl.program_id(0) == 0)
    def _():
        lse, taken, target, raw, factor = (st[i : i + 1, :] for i in range(5))
        probs[...] = (jnp.exp(lt[...] - lse) * factor).astype(BF)
        rows = MB * MROWS

        def chosen(ref):
            a, b = ref[0:1, :], ref[1:2, :]
            return jnp.concatenate([a + (b - a) * order[m] for m in range(MB)], axis=1).astype(F32)

        reward, finished = chosen(rewards), chosen(done)
        lane = lax.broadcasted_iota(jnp.int32, (1, rows), 1)
        following = jnp.where(lane % WIN == WIN - 1, 0.0, pltpu.roll(raw, rows - 1, 1))
        error = taken - (0.5 * reward + GAMMA * (1.0 - finished) * following)
        gain = target - raw
        weight = jnp.where(gain < 0, 1.0 - TAU, TAU)
        for m in range(MB):
            cols = slice(m * MROWS, (m + 1) * MROWS)
            val[m : m + 1, :] = raw[:, cols]
            adv[m : m + 1, :] = gain[:, cols]
            td[m : m + 1, :] = error[:, cols]
        vloss[...] = jnp.sum(weight * gain * gain, axis=1, keepdims=True) / rows
        qloss[...] = jnp.sum(error * error + ALPHA * (lse - taken), axis=1, keepdims=True) / rows

    product = lax.dot_general(g[...], probs[...], (((1,), (1,)), ((), ())), preferred_element_type=F32)
    grad[...] = (product * (VQ * D**-0.5 / (MB * MROWS))).astype(BF)


def run_finish(order, rewards, done, g, lt, st):
    rows = MB * MROWS

    def whole(*shape):
        return pl.BlockSpec(shape, lambda i: (0,) * len(shape))

    small = jax.ShapeDtypeStruct((MB, MROWS), F32)
    one = jax.ShapeDtypeStruct((1, 1), F32)
    return pl.pallas_call(
        finish,
        name="finish",
        grid=(D // FB,),
        out_shape=(small, small, small, one, one, jax.ShapeDtypeStruct((D, CH), BF)),
        in_specs=[
            pl.BlockSpec(memory_space=pltpu.SMEM),
            whole(MB, MROWS),
            whole(MB, MROWS),
            pl.BlockSpec((FB, rows), lambda i: (i, 0)),
            whole(CH, rows),
            whole(8, rows),
        ],
        out_specs=(
            whole(MB, MROWS),
            whole(MB, MROWS),
            whole(MB, MROWS),
            whole(1, 1),
            whole(1, 1),
            pl.BlockSpec((FB, CH), lambda i: (i, 0)),
        ),
        scratch_shapes=[pltpu.VMEM((CH, rows), BF)],
        compiler_params=pltpu.CompilerParams(vmem_limit_bytes=VMEM),
    )(order, rewards, done, g, lt, st)


def local(
    inputs, layer_gain, up_weight, down_weight, final_gain, value_head,
    q_head, target_head, actions, rewards, done, order,
):
    g, lt, st = run_trunk(
        order, actions, layer_gain, final_gain, value_head,
        inputs, up_weight, down_weight, q_head, target_head,
    )
    val, adv, td, vloss, qloss, grad = run_finish(order, rewards, done, g, lt, st)
    return val, adv, td, vloss.reshape(()), qloss.reshape(()), grad


def solution(mesh):
    in_specs = (
        P(None, "dp", None),
        P("pipe", None),
        P("pipe", "dp", "tensor"),
        P("pipe", "tensor", "dp"),
        P(),
        P(),
        P(None, ("pipe", "tensor", "dp")),
        P(None, ("pipe", "tensor", "dp")),
        P(),
        P(),
        P(),
        P(),
    )
    out_specs = (P(), P(), P(), P(), P(), P(None, ("pipe", "tensor", "dp")))
    return jax.shard_map(local, mesh=mesh, in_specs=in_specs, out_specs=out_specs, check_vma=False)
```

```python
import jax
import jax.numpy as jnp
from jax import lax
from jax.experimental import pallas as pl
from jax.experimental.pallas import tpu as pltpu
from jax.sharding import PartitionSpec as P

VQ = 65536
EPS = 1e-05
GAMMA = 0.99
TAU = 0.7
ALPHA = 0.5

MB = 2
MROWS = 256
WIN = 64
NC, ROWS = 4, 128
D = 4096
DC = 1024
FT = 896
UW = 1024
NP, NT, ND, NZ = 4, 16, 4, 8
SPLIT = 32
SUB, XC = 16, 512
QA, QB = 256, 256
VMEM = 63 * 2**20
CH = 256
BF, F32 = jnp.bfloat16, jnp.float32
MESH = pl.DeviceIdType.MESH


def remote(src, dst, send, recv, dev):
    return pltpu.make_async_remote_copy(
        src_ref=src, dst_ref=dst, send_sem=send, recv_sem=recv, device_id=dev, device_id_type=MESH
    )


def loop(low, high, body):
    def step(i, carry):
        body(i)
        return carry

    lax.fori_loop(low, high, step, 0)


def trunk(
    order_any, acts_any, lgain_any, fgain_any, vhead_any, x_any, up_any, dn_any, q_any, tg_any,
    g_out, lt_any, st_out,
    order, acts, lgain, fgain, vhead, xin, xs, sbuf, upw, dnw, qv, tv, usend, urecv, hbuf, dsend, drecv, osend,
    ga, gb, gt, acc, acct, vacc, ssq, lt, own, l1, own2, l2,
    lsem, isnd, ircv, usnd, urcv, hsnd, hrcv, dsnd, drcv, ssnd, srcv,
    a1snd, a1rcv, azsnd, azrcv, axsnd, axrcv, acsnd, acrcv,
    b1snd, b1rcv, bxsnd, bxrcv, bysnd, byrcv, bcsnd, bcrcv, l1snd, l1rcv, l2snd, l2rcv,
):
    p, t, d = lax.axis_index("pipe"), lax.axis_index("tensor"), lax.axis_index("dp")
    xl, z = t // NZ, t % NZ

    def seg(i, n):
        return pl.ds(pl.multiple_of(i * n, n), n)

    loads = [
        pltpu.make_async_copy(up_any.at[0], upw, lsem.at[0]),
        pltpu.make_async_copy(dn_any.at[0], dnw, lsem.at[1]),
        pltpu.make_async_copy(q_any, qv, lsem.at[2]),
        pltpu.make_async_copy(tg_any, tv, lsem.at[3]),
        pltpu.make_async_copy(fgain_any, fgain, lsem.at[4]),
        pltpu.make_async_copy(vhead_any, vhead, lsem.at[5]),
        pltpu.make_async_copy(acts_any, acts, lsem.at[6]),
    ]
    load_x = pltpu.make_async_copy(x_any, xin, lsem.at[7])
    load_order = pltpu.make_async_copy(order_any, order, lsem.at[8])
    load_gain = pltpu.make_async_copy(lgain_any, lgain, lsem.at[9])

    def arrived(same_bytes, sem):
        pltpu.make_async_copy(same_bytes, same_bytes, sem).wait()

    def entry(m, s):
        return sbuf.at[2 * m + s // 2, seg(s % 2, WIN), :]

    def c_in(m, k):
        dd = (d + k) % ND
        return remote(xs.at[m, :, seg(dd, DC)], entry(m, d), isnd.at[0], ircv.at[m, d], (p, t, dd))

    def c_up(c, k):
        dd = (d + 1 + k % (ND - 1)) % ND
        return remote(usend.at[c, seg(dd, SPLIT), :], urecv.at[c, k], usnd.at[0], urcv.at[c], (p, t, dd))

    def c_hid(c, k):
        part = hbuf.at[c, seg(d, SPLIT), :]
        return remote(part, part, hsnd.at[0], hrcv.at[c], (p, t, (d + 1 + k % (ND - 1)) % ND))

    def tile(ref, c, tt):
        return ref.at[c, seg(tt % NZ, SUB), seg(tt // NZ, XC)]

    def peer(i):
        j = i // 2
        away = (NZ // 2 + jnp.where(j % 2 == 1, -((j + 1) // 2), j // 2)) % NZ
        return (xl + 1 + i % 2) % 2 * NZ + (z + away) % NZ

    def c_down(c, k):
        tt = peer(k)
        return remote(tile(dsend, c, tt), drecv.at[c, k], dsnd.at[0], drcv.at[c], (p, tt, d))

    def c_state(c, k):
        return remote(osend.at[c], tile(sbuf, c, t), ssnd.at[0], srcv.at[c], (lax.rem(p + 1, NP), peer(k), d))

    def a_piece(c, dd):
        return ga.at[xl, seg(c * NZ + z, SUB), seg(dd, QA)]

    def c_a1(c, k):
        dev = (jnp.where(k < ND, 3, 1), t, (d + k) % ND)
        return remote(a_piece(c, d), a_piece(c, d), a1snd.at[0], a1rcv.at[c], dev)

    def a_slab(c, b, zz):
        return ga.at[b, seg(c * NZ + zz, SUB), :]

    def c_az(c, k):
        part = a_slab(c, xl, z)
        return remote(part, part, azsnd.at[0], azrcv.at[c, z], (p, xl * NZ + (z + k) % NZ, d))

    def c_ax(c, zz):
        part = a_slab(c, xl, zz)
        return remote(part, part, axsnd.at[0], axrcv.at[c], (p, (1 - xl) * NZ + z, d))

    other_core = (p + 1 - 2 * lax.rem(p, 2), t, d)

    def c_ac(c, b, zz):
        part = a_slab(c, b, zz)
        return remote(part, part, acsnd.at[0], acrcv.at[c], other_core)

    def c_b1(c, k):
        dev = (jnp.where(k < NZ, 2, 0), xl * NZ + (z + k) % NZ, d)
        src, dst = osend.at[c, :, pl.ds(QA, QB)], gb.at[d, seg(c * NZ + z, SUB), seg(xl, QB)]
        return remote(src, dst, b1snd.at[0], b1rcv.at[c], dev)

    def b_slab(c, dd, b):
        return gb.at[dd, seg(c, ROWS), seg(b, QB)]

    def c_bx(c):
        part = b_slab(c, d, xl)
        return remote(part, part, bxsnd.at[0], bxrcv.at[c], (p, (1 - xl) * NZ + z, d))

    def c_by(c, b, k):
        part = b_slab(c, d, b)
        return remote(part, part, bysnd.at[0], byrcv.at[c, b], (p, t, (d + k) % ND))

    def c_bc(c, dd, b):
        part = b_slab(c, dd, b)
        return remote(part, part, bcsnd.at[0], bcrcv.at[c], other_core)

    def c_one(k):
        return remote(own, l1.at[k], l1snd.at[0], l1rcv.at[0], (p, peer(k), d))

    def c_two(k):
        o = (p * ND + d + k) % (NP * ND)
        return remote(own2, l2.at[k], l2snd.at[0], l2rcv.at[0], (o // ND, t, o % ND))

    def write(c):
        return pltpu.make_async_copy(gt.at[:, seg(c, ROWS)], g_out.at[:, seg(c, ROWS)], lsem.at[10 + c])

    first, last, even, odd = p == 0, p == NP - 1, lax.rem(p, 2) == 0, lax.rem(p, 2) == 1

    barrier = pltpu.get_barrier_semaphore()

    def greet(dev):
        pl.semaphore_signal(barrier, inc=1, device_id=dev, device_id_type=MESH)

    loop(0, NT - 1, lambda k: greet((p, peer(k), d)))
    loop(1, ND, lambda k: greet((p, t, (d + k) % ND)))

    @pl.when(p > 0)
    def _():
        greet((p - 1, t, d))

    load_order.start()

    @pl.when(first)
    def _():
        load_x.start()

    load_gain.start()
    for one in loads:
        one.start()

    @pl.when(p < NP - 1)
    def _():
        pl.semaphore_wait(barrier, ND + NT - 1)

    @pl.when(last)
    def _():
        pl.semaphore_wait(barrier, ND + NT - 2)

    load_order.wait()

    @pl.when(first)
    def _():
        load_x.wait()

        def enter(m):
            xs[m] = xin[order[m]]
            loop(1, ND, lambda k: c_in(m, k).start())
            sbuf[2 * m + d // 2, seg(d % 2, WIN), :] = xs[m, :, seg(d, DC)]

        loop(0, MB, enter)

    load_gain.wait()
    for one in loads:
        one.wait()

    offset = ((p * NT + t) * ND + d) * CH
    ids = offset + lax.broadcasted_iota(jnp.int32, (CH, ROWS), 0)
    vrow = vhead[...].astype(F32).reshape(1, D)

    def up(c):
        @pl.when(first)
        def _():
            for i in range(2):
                s = 2 * (c % 2) + i

                @pl.when(s != d)
                def _():
                    arrived(entry(c // 2, s), ircv.at[c // 2, s])

        @pl.when(p > 0)
        def _():
            arrived(sbuf.at[c], srcv.at[c])

        wide = sbuf[c].astype(F32)
        square = jnp.sum(wide * wide, axis=-1, keepdims=True)
        scaled = (wide * lgain[0:1, seg(d, DC)]).astype(BF)
        usend[c, :, :FT] = jnp.dot(scaled, upw[...], preferred_element_type=F32).astype(BF)
        high = square.astype(BF).astype(F32)
        lane = lax.broadcasted_iota(jnp.int32, (ROWS, UW - FT), 1)
        usend[c, :, FT:] = jnp.where(lane < (UW - FT) // 2, high, square - high).astype(BF)
        loop(1, ND, lambda k: c_up(c, k).start())

    def hidden(c):
        arrived(urecv.at[c, pl.ds(1, ND - 1)], urcv.at[c])
        total = usend[c, seg(d, SPLIT), :].astype(F32)
        for k in range(1, ND):
            total = total + urecv[c, k].astype(F32)
        square = total[:, FT : FT + 1] + total[:, (FT + UW) // 2 : (FT + UW) // 2 + 1]
        upper = total[:, :FT] * lax.rsqrt(square / D + EPS)
        hbuf[c, seg(d, SPLIT), :] = (upper / (1.0 + jnp.exp(-upper))).astype(BF)
        loop(1, ND, lambda k: c_hid(c, k).start())

    def down(c):
        arrived(hbuf.at[c, pl.ds(0, ROWS - SPLIT), :], hrcv.at[c])
        dsend[c] = jnp.dot(hbuf[c], dnw[...], preferred_element_type=F32).astype(BF)
        loop(0, NT - 1, lambda k: c_down(c, k).start())

    def reduce(c):
        arrived(drecv.at[c, pl.ds(0, NT - 1)], drcv.at[c])
        total = tile(dsend, c, t)[...].astype(F32)
        for k in range(NT - 1):
            total = total + drecv[c, k].astype(F32)
        osend[c] = (tile(sbuf, c, t)[...].astype(F32) + total).astype(BF)

        @pl.when(p < NP - 1)
        def _():
            loop(0, NT, lambda k: c_state(c, k).start())

        @pl.when(last)
        def _():
            at = seg(c * NZ + z, SUB)
            ga[xl, at, seg(d, QA)] = osend[c, :, :QA]
            loop(1, 2 * ND, lambda k: c_a1(c, k).start())
            loop(0, 2 * NZ, lambda k: c_b1(c, k).start())

    def a_across(c):
        @pl.when(last)
        def _():
            arrived(drecv.at[c, pl.ds(1, ND - 1), :, pl.ds(0, QA)], a1rcv.at[c])

        @pl.when(p == 1)
        def _():
            arrived(drecv.at[c, pl.ds(0, ND), :, pl.ds(0, QA)], a1rcv.at[c])

        loop(1, NZ, lambda k: c_az(c, k).start())
        c_ax(c, z).start()
        c_ac(c, xl, z).start()

    def a_onward(c):
        def come(k):
            zz = (z + k) % NZ
            arrived(a_slab(c, xl, zz), azrcv.at[c, zz])
            c_ax(c, zz).start()
            c_ac(c, xl, zz).start()

        loop(1, NZ, come)

    def a_landing(c):
        part = ga.at[1 - xl, seg(c, ROWS), :]
        arrived(part, axrcv.at[c])
        remote(part, part, acsnd.at[0], acrcv.at[c], other_core).start()

    def b_across(c):
        arrived(drecv.at[c, pl.ds(0, NZ), :, pl.ds(0, QB)], b1rcv.at[c])
        c_bx(c).start()
        loop(1, ND, lambda k: c_by(c, xl, k).start())
        c_bc(c, d, xl).start()

    def b_onward(c):
        arrived(b_slab(c, d, 1 - xl), bxrcv.at[c])
        loop(1, ND, lambda k: c_by(c, 1 - xl, k).start())
        c_bc(c, d, 1 - xl).start()

    def b_landing(c):
        def come(b):
            arrived(gb.at[pl.ds(1, ND - 1), seg(c, ROWS), seg(b, QB)], byrcv.at[c, b])
            loop(1, ND, lambda k: c_bc(c, (d + k) % ND, b).start())

        come(xl)
        come(1 - xl)

    def folded(block):
        return sum(block[:, i * 128 : (i + 1) * 128] for i in range(XC // 128))

    def head(c):
        @pl.when(even)
        def _():
            arrived(ga.at[:, seg(c, ROWS), :], acrcv.at[c])

        @pl.when(odd)
        def _():
            arrived(gb.at[:, seg(c, ROWS), :], bcrcv.at[c])

        rows = seg(c, ROWS)
        for i in range(2 * ND):
            b, dd = i % 2, i // 2
            cols = slice(i * XC, (i + 1) * XC)
            wide = jnp.concatenate(
                [ga[b, rows, dd * QA : (dd + 1) * QA], gb[dd, rows, b * QB : (b + 1) * QB]], axis=1
            ).astype(F32)
            scaled = (wide * fgain[cols].reshape(1, XC)).astype(BF)
            gt[cols, rows] = scaled.T
            part = jnp.dot(scaled, qv[cols, :], preferred_element_type=F32)
            tpart = jnp.dot(scaled, tv[cols, :], preferred_element_type=F32)
            vpart = folded(scaled.astype(F32) * vrow[:, cols])
            square = folded(wide * wide)
            if i == 0:
                acc[...], acct[...], vacc[...], ssq[...] = part, tpart, vpart, square
            else:
                acc[...] += part
                acct[...] += tpart
                vacc[...] += vpart
                ssq[...] += square
        write(c).start()
        factor = lax.rsqrt(jnp.sum(ssq[...].T, axis=0, keepdims=True) / D + EPS)
        small = factor * D**-0.5
        logits = acc[...].T * small
        target = acct[...].T * small
        where = seg(c % 2, ROWS)
        action = acts[0:1, where] + (acts[1:2, where] - acts[0:1, where]) * order[c // 2]
        hit = ids == action
        top = jnp.max(logits, axis=0, keepdims=True)
        lt[:, rows] = logits
        own[0:1, rows] = top + jnp.log(jnp.sum(jnp.exp(logits - top), axis=0, keepdims=True))
        own[1:2, rows] = jnp.sum(jnp.where(hit, logits, 0.0), axis=0, keepdims=True)
        own[2:3, rows] = jnp.sum(jnp.where(hit, target, 0.0), axis=0, keepdims=True)
        own[3:4, rows] = jnp.zeros((1, ROWS), F32)
        st_out[3:4, rows] = jnp.sum(vacc[...].T, axis=0, keepdims=True) * small
        st_out[4:5, rows] = factor

    shift = jnp.where(last, 0, 2)

    def wave(s):
        def stage(c, body, here=True):
            @pl.when((c >= 0) & (c < NC) & here)
            def _():
                body(c)

        stage(s - 2, hidden)
        stage(s - 3, down)
        stage(s - 5, reduce)
        stage(s, up)
        stage(s - 8 - shift, a_onward, odd)
        stage(s - 9 - shift, a_landing, odd)
        stage(s - 6 - shift, a_across, odd)
        stage(s - 6 - shift, b_across, even)
        stage(s - 7 - shift, b_onward, even)
        stage(s - 8 - shift, b_landing, even)
        stage(s - 10 - shift, head)

    loop(0, NC + 12, wave)
    leave = pltpu.make_async_copy(lt, lt_any, lsem.at[10 + NC])
    leave.start()

    def combined(parts):
        top = jnp.max(parts, axis=0)
        merged = top + jnp.log(jnp.sum(jnp.exp(parts - top[None]), axis=0))
        row = lax.broadcasted_iota(jnp.int32, top.shape, 0)
        return jnp.where(row == 0, merged, jnp.sum(parts, axis=0))

    loop(0, NT - 1, lambda k: c_one(k).start())
    l1[NT - 1] = own[...]
    arrived(l1.at[pl.ds(0, NT - 1)], l1rcv.at[0])
    own2[...] = combined(l1[...])
    loop(1, NP * ND, lambda k: c_two(k).start())
    l2[0] = own2[...]
    arrived(l2.at[pl.ds(1, NP * ND - 1)], l2rcv.at[0])
    everywhere = combined(l2[...])
    st_out[0:3, :] = everywhere[0:3, :]
    st_out[5:8, :] = jnp.zeros((3, MB * MROWS), F32)

    @pl.when(first)
    def _():
        arrived(xs.at[:, :, pl.ds(0, (ND - 1) * DC)], isnd.at[0])

    arrived(urecv.at[:, pl.ds(1, ND - 1)], usnd.at[0])
    arrived(hbuf.at[:, pl.ds(0, ROWS - SPLIT), :], hsnd.at[0])
    arrived(drecv.at[:, pl.ds(1, NT - 1)], dsnd.at[0])

    @pl.when(p < NP - 1)
    def _():
        arrived(drecv, ssnd.at[0])

    @pl.when(last)
    def _():
        arrived(drecv.at[:, pl.ds(1, 2 * ND - 1), :, pl.ds(0, QA)], a1snd.at[0])
        arrived(drecv.at[:, :, :, pl.ds(0, QB)], b1snd.at[0])

    @pl.when(odd)
    def _():
        arrived(ga.at[0, pl.ds(0, NC * (NZ - 1) * SUB), :], azsnd.at[0])
        arrived(ga.at[0], axsnd.at[0])
        arrived(ga, acsnd.at[0])

    @pl.when(even)
    def _():
        arrived(gb.at[0, :, pl.ds(0, QB)], bxsnd.at[0])
        arrived(gb.at[pl.ds(1, ND - 1)], bysnd.at[0])
        arrived(gb, bcsnd.at[0])

    loop(0, NC, lambda c: write(c).wait())
    leave.wait()
    arrived(l1.at[pl.ds(1, NT - 1)], l1snd.at[0])
    arrived(l2.at[pl.ds(1, NP * ND - 1)], l2snd.at[0])


def run_trunk(order, acts, lgain, fgain, vhead, x, up, dn, q, tg):
    vm, anyw = pl.BlockSpec(memory_space=pltpu.VMEM), pl.BlockSpec(memory_space=pl.ANY)
    dma = pltpu.SemaphoreType.DMA
    rows = MB * MROWS
    return pl.pallas_call(
        trunk,
        name="trunk",
        out_shape=(
            jax.ShapeDtypeStruct((D, rows), BF),
            jax.ShapeDtypeStruct((CH, rows), F32),
            jax.ShapeDtypeStruct((8, rows), F32),
        ),
        in_specs=[anyw] * 10,
        out_specs=(anyw, anyw, vm),
        scratch_shapes=[
            pltpu.SMEM((MB,), jnp.int32),
            pltpu.VMEM((MB, MROWS), jnp.int32),
            pltpu.VMEM((1, D), F32),
            pltpu.VMEM((D,), F32),
            pltpu.VMEM((D,), BF),
            pltpu.VMEM((MB, WIN, D), BF),
            pltpu.VMEM((MB, WIN, D), BF),
            pltpu.VMEM((NC, ROWS, DC), BF),
            pltpu.VMEM((DC, FT), BF),
            pltpu.VMEM((FT, DC), BF),
            pltpu.VMEM((D, CH), BF),
            pltpu.VMEM((D, CH), BF),
            pltpu.VMEM((NC, ROWS, UW), BF),
            pltpu.VMEM((NC, ND, SPLIT, UW), BF),
            pltpu.VMEM((NC, ROWS, FT), BF),
            pltpu.VMEM((NC, ROWS, DC), BF),
            pltpu.VMEM((NC, NT, SUB, XC), BF),
            pltpu.VMEM((NC, SUB, XC), BF),
            pltpu.VMEM((2, rows, ND * QA), BF),
            pltpu.VMEM((ND, rows, 2 * QB), BF),
            pltpu.VMEM((D, rows), BF),
            pltpu.VMEM((ROWS, CH), F32),
            pltpu.VMEM((ROWS, CH), F32),
            pltpu.VMEM((ROWS, 128), F32),
            pltpu.VMEM((ROWS, 128), F32),
            pltpu.VMEM((CH, rows), F32),
            pltpu.VMEM((4, rows), F32),
            pltpu.VMEM((NT, 4, rows), F32),
            pltpu.VMEM((4, rows), F32),
            pltpu.VMEM((NP * ND, 4, rows), F32),
            dma((11 + NC,)),
            dma((1,)), dma((MB, ND)),
            dma((1,)), dma((NC,)),
            dma((1,)), dma((NC,)),
            dma((1,)), dma((NC,)),
            dma((1,)), dma((NC,)),
            dma((1,)), dma((NC,)),
            dma((1,)), dma((NC, NZ)),
            dma((1,)), dma((NC,)),
            dma((1,)), dma((NC,)),
            dma((1,)), dma((NC,)),
            dma((1,)), dma((NC,)),
            dma((1,)), dma((NC, 2)),
            dma((1,)), dma((NC,)),
            dma((1,)), dma((1,)),
            dma((1,)), dma((1,)),
        ],
        compiler_params=pltpu.CompilerParams(collective_id=0, has_side_effects=True, vmem_limit_bytes=VMEM),
    )(order, acts, lgain, fgain, vhead, x, up, dn, q, tg)


FB = 2048


def finish(order, rewards, done, g, lt, st, val, adv, td, vloss, qloss, grad, probs):
    @pl.when(pl.program_id(0) == 0)
    def _():
        lse, taken, target, raw, factor = (st[i : i + 1, :] for i in range(5))
        probs[...] = (jnp.exp(lt[...] - lse) * factor).astype(BF)
        rows = MB * MROWS

        def chosen(ref):
            a, b = ref[0:1, :], ref[1:2, :]
            return jnp.concatenate([a + (b - a) * order[m] for m in range(MB)], axis=1).astype(F32)

        reward, finished = chosen(rewards), chosen(done)
        lane = lax.broadcasted_iota(jnp.int32, (1, rows), 1)
        following = jnp.where(lane % WIN == WIN - 1, 0.0, pltpu.roll(raw, rows - 1, 1))
        error = taken - (0.5 * reward + GAMMA * (1.0 - finished) * following)
        gain = target - raw
        weight = jnp.where(gain < 0, 1.0 - TAU, TAU)
        for m in range(MB):
            cols = slice(m * MROWS, (m + 1) * MROWS)
            val[m : m + 1, :] = raw[:, cols]
            adv[m : m + 1, :] = gain[:, cols]
            td[m : m + 1, :] = error[:, cols]
        vloss[...] = jnp.sum(weight * gain * gain, axis=1, keepdims=True) / rows
        qloss[...] = jnp.sum(error * error + ALPHA * (lse - taken), axis=1, keepdims=True) / rows

    product = lax.dot_general(g[...], probs[...], (((1,), (1,)), ((), ())), preferred_element_type=F32)
    grad[...] = (product * (VQ * D**-0.5 / (MB * MROWS))).astype(BF)


def run_finish(order, rewards, done, g, lt, st):
    rows = MB * MROWS

    def whole(*shape):
        return pl.BlockSpec(shape, lambda i: (0,) * len(shape))

    small = jax.ShapeDtypeStruct((MB, MROWS), F32)
    one = jax.ShapeDtypeStruct((1, 1), F32)
    return pl.pallas_call(
        finish,
        name="finish",
        grid=(D // FB,),
        out_shape=(small, small, small, one, one, jax.ShapeDtypeStruct((D, CH), BF)),
        in_specs=[
            pl.BlockSpec(memory_space=pltpu.SMEM),
            whole(MB, MROWS),
            whole(MB, MROWS),
            pl.BlockSpec((FB, rows), lambda i: (i, 0)),
            whole(CH, rows),
            whole(8, rows),
        ],
        out_specs=(
            whole(MB, MROWS),
            whole(MB, MROWS),
            whole(MB, MROWS),
            whole(1, 1),
            whole(1, 1),
            pl.BlockSpec((FB, CH), lambda i: (i, 0)),
        ),
        scratch_shapes=[pltpu.VMEM((CH, rows), BF)],
        compiler_params=pltpu.CompilerParams(vmem_limit_bytes=VMEM),
    )(order, rewards, done, g, lt, st)


def local(
    inputs, layer_gain, up_weight, down_weight, final_gain, value_head,
    q_head, target_head, actions, rewards, done, order,
):
    g, lt, st = run_trunk(
        order, actions, layer_gain, final_gain, value_head,
        inputs, up_weight, down_weight, q_head, target_head,
    )
    val, adv, td, vloss, qloss, grad = run_finish(order, rewards, done, g, lt, st)
    return val, adv, td, vloss.reshape(()), qloss.reshape(()), grad


def solution(mesh):
    in_specs = (
        P(None, "dp", None),
        P("pipe", None),
        P("pipe", "dp", "tensor"),
        P("pipe", "tensor", "dp"),
        P(),
        P(),
        P(None, ("pipe", "tensor", "dp")),
        P(None, ("pipe", "tensor", "dp")),
        P(),
        P(),
        P(),
        P(),
    )
    out_specs = (P(), P(), P(), P(), P(), P(None, ("pipe", "tensor", "dp")))
    return jax.shard_map(local, mesh=mesh, in_specs=in_specs, out_specs=out_specs, check_vma=False)
```
